128 devices in a mesh: dp: 32 (over y, z_lo, x), mp: 4 (over z_hi, core).
Axes of the slice: x: 4, y: 4, z: 4 (z_hi: 2, z_lo: 2; z = z_hi * 2 + z_lo), core: 2. Of those that a mesh axis runs over, the one named last changes fastest.
Arguments:
- tags: bfloat16 [512, 128, 512], P('mp', 'dp'), may hold values from -6 to 6
- memory: bfloat16 [784, 128, 512], P('mp', 'dp'), may hold values from -6 to 6
- cotangent: bfloat16 [512, 128, 512], P('mp', 'dp'), may hold values from -6 to 6
- tag_lengths: int32 [128], P('dp'), may hold values from 64 to 512, as said below
- mem_lengths: int32 [128], P('dp'), may hold values from 392 to 784, as said below
- self_qkv: bfloat16 [512, 3, 512], P(None, None, 'mp'), may hold values from -0.25 to 0.25
- self_qv_bias: bfloat16 [2, 512], P(None, 'mp'), may hold values from -3 to 3
- self_out: bfloat16 [512, 512], P('mp'), may hold values from -2 to 2
- cross_q: bfloat16 [512, 512], P(None, 'mp'), may hold values from -0.25 to 0.25
- cross_kv: bfloat16 [512, 2, 512], P(None, None, 'mp'), may hold values from -0.25 to 0.25
- cross_qv_bias: bfloat16 [2, 512], P(None, 'mp'), may hold values from -3 to 3
- cross_out: bfloat16 [512, 512], P('mp'), may hold values from -2 to 2
- ffn_in: bfloat16 [512, 1024], P(None, 'mp'), may hold values from -0.25 to 0.25
- ffn_in_bias: bfloat16 [1024], P('mp'), may hold values from -3 to 3
- ffn_out: bfloat16 [1024, 512], P('mp'), may hold values from -0.25 to 0.25
- out_bias: bfloat16 [3, 512], replicated, may hold values from -3 to 3
- norm_gain: bfloat16 [3, 512], replicated, may hold values from 0.25 to 1.75
- norm_bias: bfloat16 [3, 512], replicated, may hold values from -3 to 3
Outputs:
- result: bfloat16 [512, 128, 512], P('mp', 'dp')
- tags_grad: bfloat16 [512, 128, 512], P('mp', 'dp')
- memory_grad: bfloat16 [784, 128, 512], P('mp', 'dp')
- grad_self_qkv: float32 [512, 3, 512], P(None, None, 'mp')
- grad_self_qv_bias: float32 [2, 512], P(None, 'mp')
- grad_self_out: float32 [512, 512], P('mp')
- grad_cross_q: float32 [512, 512], P(None, 'mp')
- grad_cross_kv: float32 [512, 2, 512], P(None, None, 'mp')
- grad_cross_qv_bias: float32 [2, 512], P(None, 'mp')
- grad_cross_out: float32 [512, 512], P('mp')
- grad_ffn_in: float32 [512, 1024], P(None, 'mp')
- grad_ffn_in_bias: float32 [1024], P('mp')
- grad_ffn_out: float32 [1024, 512], P('mp')
- grad_out_bias: float32 [3, 512], P(None, 'mp')
- grad_norm_gain: float32 [3, 512], P(None, 'mp')
- grad_norm_bias: float32 [3, 512], P(None, 'mp')
The draws below stay inside these ranges and needn't reach their ends.
Inputs may be any that keep to these rules, and one draw needn't show every extreme that they name: `tag_lengths`: per table the number of real tags; in each aligned block of 4 tables (the tables of one index of dp) one table has exactly 512. `mem_lengths`: per table the number of valid memory tokens; in each aligned block of 4 tables one table has exactly 784.
All inputs are finite; a program needn't handle non-finite values.
Results may differ from the reference program's by a relative error of at most 0.04.
Values may be sent and summed in bfloat16 or wider, within the bound.
A program may use at most 128 MiB of HBM per device.

```python
import math
import jax
import jax.numpy as jnp
from jax import lax

D = 512
HEADS = 4
HEAD = 128
FF = 1024
L = 512
MEM = 784
TAB = 4
TABLES = 128


def draw_tag_lengths(key, part):
    key = jax.random.fold_in(key, 11)
    first_key, second_key = jax.random.split(key)
    lengths_drawn = jax.random.randint(first_key, (TABLES,), L // 8, L + 1)
    chosen = jax.random.randint(second_key, (TABLES // TAB, 1), 0, TAB)
    table_slot = jnp.arange(TAB)[None, :]
    grouped = jnp.where(table_slot == chosen, L, lengths_drawn.reshape(TABLES // TAB, TAB))
    return grouped.reshape(TABLES).astype(jnp.int32)


def draw_mem_lengths(key, part):
    key = jax.random.fold_in(key, 23)
    first_key, second_key = jax.random.split(key)
    lengths_drawn = jax.random.randint(first_key, (TABLES,), MEM // 2, MEM + 1)
    chosen = jax.random.randint(second_key, (TABLES // TAB, 1), 0, TAB)
    table_slot = jnp.arange(TAB)[None, :]
    grouped = jnp.where(table_slot == chosen, MEM, lengths_drawn.reshape(TABLES // TAB, TAB))
    return grouped.reshape(TABLES).astype(jnp.int32)


def shard_levels(key, shape, cuts, smallest, high):
    loudness, own = 1.0, jax.random.fold_in(key, 6)
    for axis_at, shards_of in cuts:
        steps = jnp.exp(jax.random.uniform(jax.random.fold_in(own, axis_at), (shards_of,), jnp.float32, smallest / len(cuts), high / len(cuts)))
        loudness = loudness * jnp.repeat(steps, shape[axis_at] // shards_of).reshape([-1 if axis == axis_at else 1 for axis in range(len(shape))])
    return loudness


def bell_draw(own_key, dims, spread, reach, shards=(), dtype=jnp.bfloat16):
    values = spread * jax.random.normal(own_key, dims, jnp.float32)
    if shards:
        values = values * shard_levels(own_key, dims, shards, -0.22, 0.18)
    return jnp.clip(values, -reach, reach).astype(dtype)


def setup_inputs(seed: int = 0) -> dict:
    streams_of = jax.random.split(jax.random.key(seed), 19)
    return {
        "tags": bell_draw(streams_of[0], (L, TABLES, D), 1.0, 6.0, ((0, 4), (1, 32))),
        "memory": bell_draw(streams_of[1], (MEM, TABLES, D), 1.0, 6.0, ((0, 4), (1, 32))),
        "cotangent": bell_draw(streams_of[2], (L, TABLES, D), 1.0, 6.0, ((0, 4), (1, 32))),
        "tag_lengths": draw_tag_lengths(jax.random.fold_in(streams_of[18], 71), 0),
        "mem_lengths": draw_mem_lengths(jax.random.fold_in(streams_of[18], 71), 0),
        "self_qkv": bell_draw(streams_of[5], (D, 3, D), D ** -0.5, 0.25, ((2, 4),)),
        "self_qv_bias": bell_draw(streams_of[6], (2, D), 0.5, 3.0, ((1, 4),)),
        "self_out": bell_draw(streams_of[7], (D, D), (D // 64) ** -0.5, 2.0, ((0, 4),)),
        "cross_q": bell_draw(streams_of[8], (D, D), D ** -0.5, 0.25, ((1, 4),)),
        "cross_kv": bell_draw(streams_of[9], (D, 2, D), D ** -0.5, 0.25, ((2, 4),)),
        "cross_qv_bias": bell_draw(streams_of[10], (2, D), 0.5, 3.0, ((1, 4),)),
        "cross_out": bell_draw(streams_of[11], (D, D), (D // 64) ** -0.5, 2.0, ((0, 4),)),
        "ffn_in": bell_draw(streams_of[12], (D, FF), D ** -0.5, 0.25, ((1, 4),)),
        "ffn_in_bias": bell_draw(streams_of[13], (FF,), 0.5, 3.0, ((0, 4),)),
        "ffn_out": bell_draw(streams_of[14], (FF, D), (FF // 2) ** -0.5, 0.25, ((0, 4),)),
        "out_bias": bell_draw(streams_of[15], (3, D), 0.5, 3.0),
        "norm_gain": jnp.clip(1.0 + 0.15 * jax.random.normal(streams_of[16], (3, D), jnp.float32), 0.25, 1.75).astype(jnp.bfloat16),
        "norm_bias": bell_draw(streams_of[17], (3, D), 0.5, 3.0),
    }


EPSILON = 1e-05
HIGHEST = lax.Precision.HIGHEST

@jax.custom_vjp
def low(v):
    return lax.optimization_barrier(v.astype(jnp.bfloat16)).astype(jnp.float32)

@jax.custom_vjp
def low_back(v):
    return v

def low_keep(v):
    return (low(v), None)

def low_pass(kept, grad):
    return (grad,)

def back_keep(v):
    return (v, None)

def back_low(kept, grad):
    return (low(grad),)
low.defvjp(low_keep, low_pass)
low_back.defvjp(back_keep, back_low)

def shrink_both(values):
    return low_back(low(values))

def layer_norm(values, gain_row, shift_row):
    center = values - lax.optimization_barrier(jnp.mean(values, axis=-1, keepdims=True))
    inverse = lax.rsqrt(lax.optimization_barrier(jnp.mean(center * center, axis=-1, keepdims=True)) + EPSILON)
    return center * inverse * gain_row + shift_row

def attention(queries, key_rows, values, allowed):
    scale_factor = 1.0 / math.sqrt(HEAD)
    scores = low_back(jnp.einsum('qbhe,kbhe->bhqk', queries, key_rows, precision=HIGHEST) * scale_factor)
    scores = jnp.where(allowed, scores, -1e+30)
    row_peak = lax.optimization_barrier(jnp.max(scores, axis=-1, keepdims=True))
    exp_scores = jnp.exp(scores - row_peak)
    attn_probs = low(exp_scores / lax.optimization_barrier(jnp.sum(exp_scores, axis=-1, keepdims=True)))
    return jnp.einsum('bhqk,kbhe->qbhe', attn_probs, values, precision=HIGHEST)

def table_block(weights, tag_rows, mem_rows, tag_count, mem_count):
    self_qkv, self_qv_bias, self_out, cross_q, cross_kv, cross_qv_bias, cross_out, ffn_in, ffn_in_bias, ffn_out, out_bias, norm_gain, norm_bias = weights
    seq_len, tables, model_width = tag_rows.shape
    mem_len = mem_rows.shape[0]

    def split_heads(values):
        return values.reshape(values.shape[0], tables, HEADS, HEAD)

    def join_heads(values):
        return values.reshape(values.shape[0], tables, model_width)
    positions = jnp.arange(seq_len)
    causal = positions[None, :] <= positions[:, None]
    live_keys = positions[None, :] < tag_count[:, None]
    self_allowed = causal[None, None, :, :] & live_keys[:, None, None, :]
    cross_allowed = (jnp.arange(mem_len)[None, :] < mem_count[:, None])[:, None, None, :]
    projected = jnp.einsum('lbd,dch->lbch', tag_rows, self_qkv, precision=HIGHEST)
    self_query = shrink_both(projected[:, :, 0] + self_qv_bias[0])
    self_key = shrink_both(projected[:, :, 1])
    self_value = shrink_both(projected[:, :, 2] + self_qv_bias[1])
    self_mixed = shrink_both(join_heads(attention(split_heads(self_query), split_heads(self_key), split_heads(self_value), self_allowed)))
    attended = low_back(jnp.einsum('lbh,hd->lbd', self_mixed, self_out, precision=HIGHEST))
    first_norm = layer_norm(tag_rows + attended + out_bias[0], norm_gain[0], norm_bias[0])
    cross_query = shrink_both(jnp.einsum('lbd,dh->lbh', low(first_norm), cross_q, precision=HIGHEST) + cross_qv_bias[0])
    mem_proj = jnp.einsum('mbd,dch->mbch', mem_rows, cross_kv, precision=HIGHEST)
    cross_key = shrink_both(mem_proj[:, :, 0])
    cross_value = shrink_both(mem_proj[:, :, 1] + cross_qv_bias[1])
    cross_mixed = shrink_both(join_heads(attention(split_heads(cross_query), split_heads(cross_key), split_heads(cross_value), cross_allowed)))
    crossed = low_back(jnp.einsum('lbh,hd->lbd', cross_mixed, cross_out, precision=HIGHEST))
    second_norm = layer_norm(first_norm + crossed + out_bias[1], norm_gain[1], norm_bias[1])
    pre_act = low_back(jnp.einsum('lbd,df->lbf', low(second_norm), ffn_in, precision=HIGHEST) + ffn_in_bias)
    hidden = low(jax.nn.gelu(pre_act))
    ffn_term = low_back(jnp.einsum('lbf,fd->lbd', hidden, ffn_out, precision=HIGHEST))
    return layer_norm(second_norm + ffn_term + out_bias[2], norm_gain[2], norm_bias[2])

def layer_forward(tag_values, mem_values, weights, tag_lengths, mem_lengths):
    block_size = math.gcd(TABLES, max(1, 4096 // L))
    block_count = TABLES // block_size

    def split_tables(values):
        return jnp.moveaxis(values.reshape(values.shape[0], block_count, block_size, D), 1, 0)

    def run_block(pieces):
        return table_block(weights, pieces[0], pieces[1], pieces[2], pieces[3])
    outputs = lax.map(jax.checkpoint(run_block), (split_tables(tag_values), split_tables(mem_values), tag_lengths.reshape(block_count, block_size), mem_lengths.reshape(block_count, block_size)))
    return jnp.moveaxis(outputs, 0, 1).reshape(L, TABLES, D)

def reference(tags, memory, cotangent, tag_lengths, mem_lengths, self_qkv, self_qv_bias, self_out, cross_q, cross_kv, cross_qv_bias, cross_out, ffn_in, ffn_in_bias, ffn_out, out_bias, norm_gain, norm_bias):
    weights = tuple((member.astype(jnp.float32) for member in (self_qkv, self_qv_bias, self_out, cross_q, cross_kv, cross_qv_bias, cross_out, ffn_in, ffn_in_bias, ffn_out, out_bias, norm_gain, norm_bias)))

    def whole_layer(tag_values, mem_values, weight_values):
        return layer_forward(tag_values, mem_values, weight_values, tag_lengths, mem_lengths)
    result, pullback = jax.vjp(whole_layer, tags.astype(jnp.float32), memory.astype(jnp.float32), weights)
    tag_grad, mem_grad, weight_grads = pullback(cotangent.astype(jnp.float32))
    grad_self_qkv, grad_self_qv_bias, grad_self_out, grad_cross_q, grad_cross_kv, grad_cross_qv_bias, grad_cross_out, grad_ffn_in, grad_ffn_in_bias, grad_ffn_out, grad_out_bias, grad_norm_gain, grad_norm_bias = weight_grads
    return (result.astype(jnp.bfloat16), tag_grad.astype(jnp.bfloat16), mem_grad.astype(jnp.bfloat16), grad_self_qkv, grad_self_qv_bias, grad_self_out, grad_cross_q, grad_cross_kv, grad_cross_qv_bias, grad_cross_out, grad_ffn_in, grad_ffn_in_bias, grad_ffn_out, grad_out_bias, grad_norm_gain, grad_norm_bias)
```

```python
import math

import jax
import jax.numpy as jnp
from jax import lax
from jax.experimental import pallas as pl
from jax.experimental.pallas import tpu as pltpu
from jax.sharding import PartitionSpec as P

BF = jnp.bfloat16
F32 = jnp.float32
D = 512
HEADS = 4
HEAD = 128
L = 512
MLOC = 196
MPAD = 208
MT = 4 * MPAD
QB = 256
EPSILON = 1e-05
SCALE = 1.0 / math.sqrt(HEAD)
LOG2E = math.log2(math.e)
NEG = -1e30


def mm(a, b):
    return jnp.dot(a, b, preferred_element_type=F32)


def mm_nt(a, b):
    return lax.dot_general(a, b, (((1,), (1,)), ((), ())), preferred_element_type=F32)


def mm_tn(a, b):
    return lax.dot_general(a, b, (((0,), (0,)), ((), ())), preferred_element_type=F32)


def col_weight(w, unit):
    return jnp.concatenate([w[s, unit] for s in range(4)], axis=1)


def row_block(w, s, unit):
    return jnp.concatenate([w[s, unit, pl.ds(j * 128, 128), :] for j in range(4)], axis=1)


def row_weight(w, unit):
    return jnp.concatenate([row_block(w, s, unit) for s in range(4)], axis=0)


def put_cols(g, unit, value):
    for s in range(4):
        g[s // 2, s % 2, unit] = value[:, s * 128 : (s + 1) * 128].astype(BF)


def put_rows(g, s, unit, value):
    for j in range(4):
        g[s // 2, s % 2, unit, pl.ds(j * 128, 128), :] = value[:, j * 128 : (j + 1) * 128].astype(BF)


def norm_rows(v):
    center = v - jnp.mean(v, axis=-1, keepdims=True)
    inverse = lax.rsqrt(jnp.mean(center * center, axis=-1, keepdims=True) + EPSILON)
    return center * inverse, inverse


def norm_back(e, unit, inverse, gain):
    scaled = e * gain
    return inverse * (
        scaled
        - jnp.mean(scaled, axis=-1, keepdims=True)
        - unit * jnp.mean(scaled * unit, axis=-1, keepdims=True)
    )


def norm_back_rows(r, n, e, unit, inverse):
    gain = r.pvec[pl.ds(3 + n, 1), :]
    totals = [jnp.zeros((8, D), F32)] * 3
    for i in range(L // 128):
        rows = slice(i * 128, (i + 1) * 128)
        ei, ui = e[rows, :].astype(F32), unit[rows, :]
        di = norm_back(ei, ui, inverse[rows, :], gain)
        yield rows, di
        parts = (di, ei * ui, ei)
        totals = [t + jnp.sum(v.reshape(16, 8, D), axis=0) for t, v in zip(totals, parts)]
    for j in range(3):
        r.sums[pl.ds(3 * j + n, 1), :] = jnp.sum(totals[j], axis=0, keepdims=True)


GELU_C = math.sqrt(2.0 / math.pi)


def gelu_both(z):
    z2 = z * z
    t = jnp.tanh(GELU_C * z * (1.0 + 0.044715 * z2))
    half = 0.5 * (1.0 + t)
    return z * half, half + (0.5 * GELU_C) * z * (1.0 - t * t) * (1.0 + 3 * 0.044715 * z2)


def col_sum(v):
    return jnp.sum(v, axis=0, keepdims=True)


def bias_row(small, row):
    return jnp.concatenate([small[s, pl.ds(row, 1), :] for s in range(4)], axis=1)


def head_rows(h):
    return pl.ds(h * HEAD if isinstance(h, int) else pl.multiple_of(h * HEAD, HEAD), HEAD)


def attend(q, k, v, p, ot, rinv, sbuf, keybias, causal, limit, key_block, heads):
    items = [(h, qb) for h in heads for qb in range(L // QB)]
    peaks, totals = {}, {}

    def score(i, kb):
        h, qb = items[i]
        rows = pl.ds(kb * key_block, key_block)
        s = mm_nt(k[h, rows, :], q[h, pl.ds(qb * QB, QB), :])
        s = s + jnp.concatenate([keybias[rows, :]] * (QB // 128), axis=1)
        if causal and kb == qb:
            key = lax.broadcasted_iota(jnp.int32, s.shape, 0)
            query = lax.broadcasted_iota(jnp.int32, s.shape, 1)
            s = jnp.where(key <= query, s, NEG)
        sbuf[i % 2, rows, :] = s
        top = jnp.max(s, axis=0, keepdims=True)
        peaks[i] = jnp.maximum(peaks[i], top) if kb else top

    def weigh(i, kb):
        h, qb = items[i]
        rows = pl.ds(kb * key_block, key_block)
        e = jnp.exp2(sbuf[i % 2, rows, :] * (SCALE * LOG2E) - peaks[i] * (SCALE * LOG2E))
        p[h, rows, pl.ds(qb * QB, QB)] = e.astype(BF)
        part = jnp.sum(e, axis=0, keepdims=True)
        totals[i] = totals[i] + part if kb else part

    def output(i):
        h, qb = items[i]
        cols, keys = pl.ds(qb * QB, QB), limit(qb)
        inv = 1.0 / totals[i]
        rinv[h, :, cols] = jnp.broadcast_to(inv, (8, QB))
        o = mm(v[h, pl.ds(0, keys), :].T, p[h, pl.ds(0, keys), cols])
        ot[head_rows(h), cols] = (o * inv).astype(BF)

    blocks = [limit(qb) // key_block for _, qb in items]
    for i in range(len(items) + 2):
        ahead = blocks[i] if i < len(items) else 0
        behind = blocks[i - 1] if 0 < i <= len(items) else 0
        for kb in range(max(ahead, behind)):
            if kb < ahead:
                score(i, kb)
            if kb < behind:
                weigh(i - 1, kb)
        if i > 1:
            output(i - 2)


def scaled_heads(do, grad, rinv):
    for h in range(HEADS):
        inv = rinv[h].T[:, :1]
        do[h] = (grad[:, h * HEAD : (h + 1) * HEAD] * inv).astype(BF)


def attend_grad(q, k, v, p, ot, do, dqt, dk, dsbuf, limit, key_block, pair):
    def one(h):
        kt = k[h].T
        span = head_rows(h)
        delta = jnp.sum(ot[span, :].astype(F32) * do[h].T.astype(F32), axis=0, keepdims=True)
        for qb in range(L // QB):
            cols = pl.ds(qb * QB, QB)
            keys = limit(qb)
            dov = do[h, cols, :]
            low = delta[:, qb * QB : (qb + 1) * QB]
            for kb in range(keys // key_block):
                rows = pl.ds(kb * key_block, key_block)
                dw = mm_nt(v[h, rows, :], dov)
                dsbuf[rows, cols] = (p[h, rows, cols].astype(F32) * (dw - low)).astype(BF)
            dq = mm(kt[:, :keys], dsbuf[pl.ds(0, keys), cols]) * SCALE
            dqt[span, cols] = dq.astype(BF)
        for rows, seen in seen_blocks(limit):
            dk[h, rows, :] = (mm(dsbuf[rows, seen], q[h, seen, :]) * SCALE).astype(BF)

    one(2 * pair)
    one(2 * pair + 1)


def seen_blocks(limit):
    below = 0
    for qb in range(L // QB):
        keys = limit(qb) - below
        if keys:
            yield pl.ds(below, keys), pl.ds(qb * QB, L - qb * QB)
        below = limit(qb)


def value_grad(p, do, dv, limit):
    def one(h):
        for rows, seen in seen_blocks(limit):
            dv[h, rows, :] = mm(p[h, rows, seen], do[h, seen, :]).astype(BF)

    for h in range(HEADS):
        one(h)


def scratch_list():
    v = pltpu.VMEM
    return dict(
        q=v((4, L, HEAD), BF), k=v((4, L, HEAD), BF), v=v((4, L, HEAD), BF),
        ps=v((4, L, L), BF), ots=v((D, L), BF), rs=v((4, 8, L), F32),
        h1=v((L, D), F32), h1b=v((L, D), BF), u1=v((L, D), F32), inv1=v((L, 1), F32),
        qc=v((4, L, HEAD), BF), kc=v((4, MT, HEAD), BF), vc=v((4, MT, HEAD), BF),
        pc=v((4, MT, L), BF), otc=v((D, L), BF), rc=v((4, 8, L), F32),
        h2b=v((L, D), BF), g=v((L, 2 * D), BF), dfb=v((L, D), BF), dz=v((L, 2 * D), BF),
        dr2=v((L, D), F32), da2=v((L, D), BF), doc=v((4, L, HEAD), BF),
        dkc=v((4, MT, HEAD), BF), dvc=v((4, MT, HEAD), BF), dqc=v((L, D), BF),
        sbuf=v((2, MT, QB), F32), dsbuf=v((MT, L), BF), keybias=v((MT, 128), F32),
    )


class Refs:
    def __init__(self, **kw):
        self.__dict__.update(kw)
        self.ob = self.dq = self.dqc
        self.xt = self.h2b
        self.dqt, self.dr1 = self.otc, self.h1
        self.da1, self.dos = self.da2, self.doc
        self.dk, self.dv = self.qc, self.vc.at[:, pl.ds(0, L), :]
        self.tgrad, self.mgrad = self.cot_t, self.mem_t


def stage_qkv(r, pair):
    heads = (2 * pair, 2 * pair + 1)
    for j, (dst, row) in enumerate(((r.q, 0), (r.k, None), (r.v, 1))):
        y = mm(r.x[...], jnp.concatenate([r.w[h, j] for h in heads], axis=1))
        if row is not None:
            y = y + jnp.concatenate([r.small[h, pl.ds(row, 1), :] for h in heads], axis=1)
        y = y.astype(BF)
        for i, h in enumerate(heads):
            dst[h] = y[:, i * HEAD : (i + 1) * HEAD]


def self_limit(qb):
    return (qb + 1) * QB


def stage_self_mask(r):
    key = lax.broadcasted_iota(jnp.int32, (L, 128), 0)
    r.keybias[pl.ds(0, L), :] = jnp.where(key < r.lens[pl.ds(lax.axis_index("mp"), 1), :], 0.0, NEG)


def stage_cross_mask(r):
    token = lax.broadcasted_iota(jnp.int32, (MPAD, 128), 0)
    memlen = r.lens[pl.ds(4 + lax.axis_index("mp"), 1), :]
    for i in range(4):
        seen = (token < MLOC) & (token + i * MLOC < memlen)
        r.keybias[pl.ds(i * MPAD, MPAD), :] = jnp.where(seen, 0.0, NEG)


def stage_self(r, pair):
    heads = (2 * pair, 2 * pair + 1)
    attend(r.q, r.k, r.v, r.ps, r.ots, r.rs, r.sbuf, r.keybias, True, self_limit, QB, heads)


def stage_first(r):
    r.ob[...] = r.ots[...].T
    wso = row_weight(r.w, 3)

    rows = pl.ds(0, L)
    v = r.x[rows, :].astype(F32) + mm(r.ob[rows, :], wso) + r.pvec[pl.ds(0, 1), :]
    unit, inv = norm_rows(v)
    r.u1[rows, :] = unit
    r.inv1[rows, :] = inv
    h1 = unit * r.pvec[pl.ds(3, 1), :] + r.pvec[pl.ds(6, 1), :]
    r.h1[rows, :] = h1
    r.h1b[rows, :] = h1.astype(BF)


def stage_cross_q(r):
    y = (mm(r.h1b[...], col_weight(r.w, 4)) + bias_row(r.small, 2)).astype(BF)
    for h in range(HEADS):
        r.qc[h] = y[:, h * HEAD : (h + 1) * HEAD]


def stage_cross_kv(r):
    for j, (dst, row) in enumerate(((r.kc, None), (r.vc, 3))):
        y = mm(r.m[...], col_weight(r.w, 5 + j))
        if row is not None:
            y = y + bias_row(r.small, row)
        y = y.astype(BF)
        for h in range(HEADS):
            dst[h] = y[:, h * HEAD : (h + 1) * HEAD]


def cross_limit(qb):
    return MT


def stage_cross(r):
    attend(r.qc, r.kc, r.vc, r.pc, r.otc, r.rc, r.sbuf, r.keybias, False, cross_limit, MPAD, range(HEADS))


def ffn_weights(r, s):
    w_in = jnp.concatenate([r.w[s, 8], r.w[s, 9]], axis=1)
    w_out = jnp.concatenate([row_block(r.w, s, 10), row_block(r.w, s, 11)], axis=0)
    return w_in, w_out


def stage_rows(r, cotangent_ready=lambda: None):
    r.ob[...] = r.otc[...].T

    v = r.h1[...] + mm(r.ob[...], row_weight(r.w, 7)) + r.pvec[pl.ds(1, 1), :]
    u2, inv2 = norm_rows(v)
    h2 = u2 * r.pvec[pl.ds(4, 1), :] + r.pvec[pl.ds(7, 1), :]
    h2b = h2.astype(BF)
    r.h2b[...] = h2b
    r3 = h2 + r.pvec[pl.ds(2, 1), :]
    slopes = []
    for s in range(4):
        w_in, w_out = ffn_weights(r, s)
        bias = jnp.concatenate([r.small[s, pl.ds(4, 1), :], r.small[s, pl.ds(5, 1), :]], axis=1)
        value, slope = gelu_both(mm(h2b, w_in) + bias)
        value = value.astype(BF)
        r.g[:, pl.ds(s * 256, 256)] = value
        slopes.append(slope)
        r3 = r3 + mm(value, w_out)
    u3, inv3 = norm_rows(r3)
    value = (u3 * r.pvec[pl.ds(5, 1), :] + r.pvec[pl.ds(8, 1), :]).astype(BF)
    for i in range(4):
        r.result[i] = value[i * 128 : (i + 1) * 128, :]
    cotangent_ready()
    r.dr2[...] = u2
    for rows, dr3 in norm_back_rows(r, 2, r.cot, u3, inv3):
        r.dr1[rows, :] = dr3
        r.dfb[rows, :] = dr3.astype(BF)
    return inv2, slopes


def stage_rows_back(r, kept):
    inv2, slopes = kept
    e2 = r.dr1[...]
    for s in range(4):
        w_in, w_out = ffn_weights(r, s)
        dz = (mm_nt(r.dfb[...], w_out) * slopes[s]).astype(BF)
        r.dz[:, pl.ds(s * 256, 256)] = dz
        e2 = e2 + mm_nt(dz, w_in)
    for rows, dr2 in norm_back_rows(r, 1, e2, r.dr2, inv2):
        r.dr2[rows, :] = dr2
        r.da2[rows, :] = dr2.astype(BF)
    scaled_heads(r.doc, mm_nt(r.da2[...], row_weight(r.w, 7)), r.rc)


def stage_ffn_out_grads(r):
    gt = r.g[...].T
    for s in range(4):
        y = mm(gt[s * 256 : (s + 1) * 256, :], r.dfb[...])
        for i in range(2):
            put_rows(r.grads, s, 10 + i, y[i * 128 : (i + 1) * 128, :])


def stage_ffn_grads(r):
    h2t = r.h2b[...].T
    for s in range(4):
        y = mm(h2t, r.dz[:, pl.ds(s * 256, 256)])
        r.grads[s // 2, s % 2, 8] = y[:, :128].astype(BF)
        r.grads[s // 2, s % 2, 9] = y[:, 128:].astype(BF)
        b = col_sum(r.dz[:, pl.ds(s * 256, 256)].astype(F32))
        r.bsums[s, pl.ds(4, 1), :] = b[:, :128]
        r.bsums[s, pl.ds(5, 1), :] = b[:, 128:]


def stage_cross_out_grad(r):
    y = mm(r.otc[...], r.da2[...])
    for s in range(4):
        put_rows(r.grads, s, 7, y[s * 128 : (s + 1) * 128, :])


def stage_cross_values(r):
    value_grad(r.pc, r.doc, r.dvc, cross_limit)


def stage_cross_back(r, pair):
    attend_grad(r.qc, r.kc, r.vc, r.pc, r.otc, r.doc, r.dqt, r.dkc, r.dsbuf, cross_limit, MPAD, pair)


def stage_cross_value_grads(r):
    mt = r.m[...].T
    dv = jnp.concatenate([r.dvc[h] for h in range(HEADS)], axis=1)
    put_cols(r.grads, 6, mm(mt, dv))
    b = col_sum(dv.astype(F32))
    for h in range(HEADS):
        r.bsums[h, pl.ds(3, 1), :] = b[:, h * HEAD : (h + 1) * HEAD]


def stage_cross_grads(r):
    mt = r.m[...].T
    r.dqc[...] = r.dqt[...].T
    put_cols(r.grads, 4, mm(r.h1b[...].T, r.dqc[...]))
    put_cols(r.grads, 5, mm(mt, jnp.concatenate([r.dkc[h] for h in range(HEADS)], axis=1)))
    b = col_sum(r.dqc[...].astype(F32))
    for h in range(HEADS):
        r.bsums[h, pl.ds(2, 1), :] = b[:, h * HEAD : (h + 1) * HEAD]


def stage_memory_grad(r):
    w = jnp.concatenate([col_weight(r.w, 5), col_weight(r.w, 6)], axis=1)
    parts = [d[h] for d in (r.dkc, r.dvc) for h in range(HEADS)]
    r.mgrad[...] = mm_nt(jnp.concatenate(parts, axis=1), w).astype(BF)


def stage_first_back(r):
    e1 = r.dr2[...] + mm_nt(r.dqc[...], col_weight(r.w, 4))
    for rows, dr1 in norm_back_rows(r, 0, e1, r.u1, r.inv1):
        r.dr1[rows, :] = dr1
        r.da1[rows, :] = dr1.astype(BF)
    scaled_heads(r.dos, mm_nt(r.da1[...], row_weight(r.w, 3)), r.rs)


def stage_self_out_grad(r):
    y = mm(r.ots[...], r.da1[...])
    for s in range(4):
        put_rows(r.grads, s, 3, y[s * 128 : (s + 1) * 128, :])


def stage_self_back(r, pair):
    attend_grad(r.q, r.k, r.v, r.ps, r.ots, r.dos, r.dqt, r.dk, r.dsbuf, self_limit, QB, pair)


def stage_self_values(r):
    value_grad(r.ps, r.dos, r.dv, self_limit)
    r.xt[...] = r.x[...].T
    dv = jnp.concatenate([r.dv[h] for h in range(HEADS)], axis=1)
    put_cols(r.grads, 2, mm(r.xt[...], dv))
    b = col_sum(dv.astype(F32))
    for h in range(HEADS):
        r.bsums[h, pl.ds(1, 1), :] = b[:, h * HEAD : (h + 1) * HEAD]


def stage_self_grads(r, pair):
    cols = pl.ds(pair * 256, 256)
    dq = r.dqt[cols, :].T
    r.dq[:, cols] = dq
    y = mm(r.xt[...], jnp.concatenate([dq, r.dk[2 * pair], r.dk[2 * pair + 1]], axis=1))
    b = col_sum(dq.astype(F32))
    for i in range(2):
        for j in range(2):
            r.grads[pair, i, j] = y[:, j * 256 + i * 128 : j * 256 + (i + 1) * 128].astype(BF)
        r.bsums[2 * pair + i, pl.ds(0, 1), :] = b[:, i * 128 : (i + 1) * 128]


def stage_tags_grad(r):
    w = jnp.concatenate([col_weight(r.w, j) for j in range(3)], axis=1)
    parts = [r.dq[...]] + [d[h] for d in (r.dk, r.dv) for h in range(HEADS)]
    y = (r.dr1[...] + mm_nt(jnp.concatenate(parts, axis=1), w)).astype(BF)
    for i in range(4):
        r.tgrad[i] = y[i * 128 : (i + 1) * 128, :]


MESH = pl.DeviceIdType.MESH


class Place:
    def __init__(self):
        dp, mp = lax.axis_index("dp"), lax.axis_index("mp")
        self.mp = mp
        self.x = lax.rem(dp, 4)
        self.lo = lax.rem(lax.div(dp, 4), 2)
        self.y = lax.div(dp, 8)
        self.hi = lax.div(mp, 2)
        self.core = lax.rem(mp, 2)

    def device(self, x=None, y=None, lo=None, hi=None, core=None):
        x = self.x if x is None else x
        y = self.y if y is None else y
        lo = self.lo if lo is None else lo
        hi = self.hi if hi is None else hi
        core = self.core if core is None else core
        return (y * 8 + lo * 4 + x, hi * 2 + core)

    def owner(self, t):
        return self.device(lo=1 - self.lo, hi=t // 2, core=t % 2)

    def sibling(self):
        return self.device(core=1 - self.core)

    def across(self):
        return self.device(lo=1 - self.lo, hi=1 - self.hi)

    def x_at(self, n):
        return lax.rem(self.x + n, 4)

    def y_at(self, n):
        return lax.rem(self.y + n, 4)

    def along(self, axis, n):
        return self.device(x=self.x_at(n)) if axis == 0 else self.device(y=self.y_at(n))

    def at(self, axis, n=0):
        return self.x_at(n) if axis == 0 else self.y_at(n)

    def peers(self):
        out = [self.owner(t) for t in range(4)]
        out.append(self.sibling())
        out.append(self.device(hi=1 - self.hi))
        for axis in range(2):
            out += [self.along(axis, n) for n in (1, 2, 3)]
        return out


class Phase:
    def __init__(self, links, view):
        self.links, self.view, self.slot, self.device = links, view, links.used, None
        links.used += 1

    def send(self, src, dst, device):
        self.device = device
        pltpu.make_async_remote_copy(
            src_ref=src,
            dst_ref=dst,
            send_sem=self.links.send_sems.at[self.slot],
            recv_sem=self.links.recv_sems.at[self.slot],
            device_id=device,
            device_id_type=MESH,
        ).start()
        if self not in self.links.started:
            self.links.started.append(self)

    def whole(self):
        return pltpu.make_async_remote_copy(
            src_ref=self.view,
            dst_ref=self.view,
            send_sem=self.links.send_sems.at[self.slot],
            recv_sem=self.links.recv_sems.at[self.slot],
            device_id=self.device,
            device_id_type=MESH,
        )

    def wait(self):
        self.whole().wait_recv()

class Links:
    def __init__(self, send_sems, recv_sems):
        self.send_sems, self.recv_sems = send_sems, recv_sems
        self.used = 0
        self.started = []

    def finish(self):
        for phase in self.started:
            phase.whole().wait_send()
        self.started = []


def greet_start(place):
    barrier = pltpu.get_barrier_semaphore()
    for peer in place.peers():
        pl.semaphore_signal(barrier, inc=1, device_id=peer, device_id_type=MESH)


def greet_wait(place):
    pl.semaphore_wait(pltpu.get_barrier_semaphore(), len(place.peers()))


class Spread:
    def __init__(self, place, links, src, dst, rows):
        self.place, self.src, self.dst, self.rows = place, src, dst, rows
        self.phase = Phase(links, dst)

    def start(self):
        p = self.place
        span = pl.ds(pl.multiple_of(p.mp * self.rows, 16), self.rows)
        for t in range(4):
            self.phase.send(table_rows(self.src, t), self.dst.at[span], p.owner(t))

    def wait(self):
        self.phase.wait()


class Collect:
    def __init__(self, place, links, src, dst):
        self.place, self.src, self.dst = place, src, dst
        self.phase = Phase(links, dst)

    def start(self):
        p = self.place
        for s in range(4):
            self.phase.send(table_rows(self.src, s), self.dst.at[p.mp], p.owner(s))

    def wait(self):
        self.phase.wait()


class Gather:
    def __init__(self, place, links, w, unit, per):
        self.place, self.w, self.unit, self.per = place, w, unit, per
        some = w.at[0]
        self.z = Phase(links, some.at[pl.ds(0, 2 * per), pl.ds(0, 32)])
        self.first = Phase(links, some.at[pl.ds(0, 2 * per), pl.ds(0, 96)])
        self.second = Phase(links, some.at[pl.ds(0, 2 * per), pl.ds(0, 384)])
        self.near, self.far = (Phase(links, some.at[pl.ds(0, 2 * per)]) for _ in range(2))

    def piece(self, shard, half, rows, count):
        units = pl.ds(self.unit + self.per * half, self.per)
        return self.w.at[shard, units, pl.ds(pl.multiple_of(rows, 32), count), :]

    def other(self):
        return (1 - self.place.hi) * 2 + self.place.core

    def row(self, half):
        p = self.place
        return p.at(1 - half) * 128 + p.at(half) * 32

    def start(self):
        p = self.place
        for half in range(2):
            view = self.piece(p.mp, half, self.row(half), 32)
            self.z.send(view, view, p.across())

    def start_near(self):
        p = self.place
        whole = self.w.at[p.mp, pl.ds(self.unit, 2 * self.per)]
        self.near.send(whole, whole, p.sibling())

    def step_first(self):
        p = self.place
        self.z.wait()
        for half in range(2):
            view = self.piece(self.other(), half, self.row(half), 32)
            for n in (1, 2, 3):
                self.first.send(view, view, p.along(half, n))

    def step_second(self):
        p = self.place
        self.first.wait()
        for half in range(2):
            view = self.piece(self.other(), half, p.at(1 - half) * 128, 128)
            for n in (1, 2, 3):
                self.second.send(view, view, p.along(1 - half, n))

    def step_last(self):
        self.second.wait()
        view = self.w.at[self.other(), pl.ds(self.unit, 2 * self.per)]
        self.far.send(view, view, self.place.sibling())


class Reduce:
    def __init__(self, place, links, r, unit, per, slots, split):
        self.place, self.r, self.unit, self.per = place, r, unit, per
        self.r1, self.b1, self.r2, self.b2, self.r3 = slots
        self.split = split
        one = r.grads.at[0, 0]
        if split:
            self.plane = [Phase(links, one.at[pl.ds(0, 2 * per), pl.ds(0, 384)]) for _ in range(2)]
        else:
            self.plane = [Phase(links, self.r1)]
        self.line, self.z = Phase(links, self.r2), Phase(links, self.r3)
        self.gather = Phase(links, one.at[pl.ds(0, 2 * per), pl.ds(0, 96)])
        self.gather_more = Phase(links, one.at[pl.ds(0, 2 * per), pl.ds(0, 384)])

    def add(self, k, unit, theirs, count):
        p, r = self.place, self.r

        def one(u, carry):
            mine = r.grads[k, p.core, unit + u].astype(F32)
            r.grads[k, p.core, unit + u] = (mine + theirs[u].astype(F32)).astype(BF)
            return carry

        lax.fori_loop(0, count, one, 0)

    def step_plane(self, k=None):
        p, r = self.place, self.r
        for half in range(2):
            units = pl.ds(self.unit + self.per * half, self.per)
            for n in (1, 2, 3):
                rows = pl.ds(pl.multiple_of(p.at(half, n) * 128, 128), 128)
                if self.split:
                    src, dst = r.grads.at[k, p.core, units, rows, :], self.r1.at[half, n - 1, k]
                else:
                    src, dst = r.grads.at[:, p.core, units, rows, :], self.r1.at[half, n - 1]
                self.plane[k if self.split else 0].send(src, dst, p.along(half, n))

    def step_line(self):
        p, r = self.place, self.r
        for phase in self.plane:
            phase.wait()
        for half in range(2):
            rows = pl.ds(pl.multiple_of(p.at(half) * 128, 128), 128)

            def one(i, carry):
                k, u = lax.div(i, self.per), lax.rem(i, self.per)
                total = r.grads[k, p.core, self.unit + self.per * half + u, rows, :].astype(F32)
                for n in range(3):
                    total = total + self.r1[half, n, k, u].astype(F32)
                self.b1[half, k, u] = total.astype(BF)
                return carry

            lax.fori_loop(0, 2 * self.per, one, 0)
            for n in (1, 2, 3):
                rows = pl.ds(pl.multiple_of(p.at(1 - half, n) * 32, 32), 32)
                src = self.b1.at[half, :, :, rows, :]
                self.line.send(src, self.r2.at[half, n - 1], p.along(1 - half, n))

    def step_z(self):
        p = self.place
        self.line.wait()
        for half in range(2):
            rows = pl.ds(pl.multiple_of(p.at(1 - half) * 32, 32), 32)
            for k in range(2):
                total = self.b1[half, k, :, rows, :].astype(F32)
                for n in range(3):
                    total = total + self.r2[half, n, k].astype(F32)
                self.b2[k, half] = total.astype(BF)
        to = (
            (p.device(lo=1 - p.lo), p.hi),
            (p.device(lo=1 - p.lo, hi=1 - p.hi), 1 - p.hi),
            (p.device(hi=1 - p.hi), 1 - p.hi),
        )
        for n, (device, hi) in enumerate(to):
            self.z.send(self.b2.at[hi], self.r3.at[n], device)

    def kept(self, half, rows, count):
        units = pl.ds(self.unit + self.per * half, self.per)
        return self.r.fin.at[units, pl.ds(pl.multiple_of(rows, 32), count), :]

    def step_spread(self):
        p = self.place
        self.z.wait()
        for half in range(2):
            near = self.b2[p.hi, half].astype(F32) + self.r3[0, half].astype(F32)
            far = self.r3[1, half].astype(F32) + self.r3[2, half].astype(F32)
            view = self.kept(half, p.at(half) * 128 + p.at(1 - half) * 32, 32)
            view[...] = (near + far).astype(BF)
            for n in (1, 2, 3):
                self.gather.send(view, view, p.along(1 - half, n))

    def step_spread_more(self):
        p = self.place
        self.gather.wait()
        for half in range(2):
            view = self.kept(half, p.at(half) * 128, 128)
            for n in (1, 2, 3):
                self.gather_more.send(view, view, p.along(half, n))

    def wait(self):
        self.gather_more.wait()


class Halves:
    def __init__(self, place, links, r, unit, landing):
        self.place, self.r, self.unit, self.landing = place, r, unit, landing
        self.count = landing[0].shape[0]
        self.phases = [Phase(links, view) for view in landing]

    def start(self, k):
        p = self.place
        src = self.r.grads.at[k, 1 - p.core, pl.ds(self.unit, self.count)]
        self.phases[k].send(src, self.landing[k], p.sibling())

    def add(self, reduce, k):
        self.phases[k].wait()
        reduce.add(k, self.unit, self.landing[k], self.count)


class SmallReduce:
    def __init__(self, place, links, r):
        self.place, self.r = place, r
        self.pair = Phase(links, r.sm0)
        self.phases = [Phase(links, slots.at[pl.ds(0, 3)]) for slots in (r.smx, r.smy, r.smz)]

    def start(self):
        p, r = self.place, self.r
        for s in range(4):
            r.sm[s % 2, s // 2, pl.ds(0, 9), :] = r.sums[pl.ds(0, 9), pl.ds(s * 128, 128)]
            r.sm[s % 2, s // 2, pl.ds(9, 6), :] = r.bsums[s, pl.ds(0, 6), :]
            r.sm[s % 2, s // 2, pl.ds(15, 1), :] = jnp.zeros((1, 128), F32)
        self.pair.send(r.sm.at[1 - p.core], r.sm0, p.sibling())

    def step_x(self):
        p, r = self.place, self.r
        self.pair.wait()
        r.smx[p.x] = r.sm[p.core] + r.sm0[...]
        for n in (1, 2, 3):
            self.phases[0].send(r.smx.at[p.x], r.smx.at[p.x], p.along(0, n))

    def step_y(self):
        p, r = self.place, self.r
        self.phases[0].wait()
        r.smy[p.y] = (r.smx[0] + r.smx[1]) + (r.smx[2] + r.smx[3])
        for n in (1, 2, 3):
            self.phases[1].send(r.smy.at[p.y], r.smy.at[p.y], p.along(1, n))

    def step_z(self):
        p, r = self.place, self.r
        self.phases[1].wait()
        mine = p.hi * 2 + p.lo
        r.smz[mine] = (r.smy[0] + r.smy[1]) + (r.smy[2] + r.smy[3])
        for lo, hi in ((1 - p.lo, p.hi), (1 - p.lo, 1 - p.hi), (p.lo, 1 - p.hi)):
            self.phases[2].send(r.smz.at[mine], r.smz.at[mine], p.device(lo=lo, hi=hi))

    def wait(self):
        p, z = self.place, self.r.smz
        self.phases[2].wait()
        total = (z[0, p.hi] + z[1, p.hi]) + (z[2, p.hi] + z[3, p.hi])
        first = 0
        for name in SMALL_OUTS:
            ref = getattr(self.r, name)
            count = ref.shape[0]
            ref[...] = total[first : first + count, :]
            first += count


SMALL_OUTS = ("gout_bias", "gnorm_gain", "gnorm_bias", "gself_qv", "gcross_qv", "gffn_bias")


class Results:
    def __init__(self, r):
        self.r, self.copies = r, []

    def put(self, src, dst):
        copy = pltpu.make_async_copy(src, dst, self.r.out_sems.at[len(self.copies)])
        copy.start()
        self.copies.append(copy)

    def rows(self, tables, pairs, dst, count=None):
        pairs[...] = jnp.swapaxes(tables[...], 0, 1)
        self.put(pairs if count is None else pairs.at[pl.ds(0, count)], dst)

    def units(self, first, count):
        span = pl.ds(first, count)
        self.put(self.r.fin.at[span], self.r.fin_out.at[span])

    def finish(self):
        for copy in self.copies:
            copy.wait()


def load_weights(r, place, sem):
    mp = place.mp
    copies = []

    def put(src, unit, rows=None, count=1):
        if rows is None:
            dst = r.w.at[mp, pl.ds(unit, count)] if count > 1 else r.w.at[mp, unit]
        else:
            dst = r.w.at[mp, unit, pl.ds(rows, 128), :]
        copy = pltpu.make_async_copy(src, dst, sem.at[len(copies)])
        copy.start()
        copies.append(copy)

    put(r.self_qkv, 0, count=3)
    for j in range(4):
        put(r.self_out.at[:, pl.ds(j * 128, 128)], 3, j * 128)
    self_count = len(copies)
    put(r.cross_q, 4)
    copy = pltpu.make_async_copy(r.cross_kv, r.kv_pairs, sem.at[len(copies)])
    copy.start()
    copies.append(copy)
    for j in range(4):
        put(r.cross_out.at[:, pl.ds(j * 128, 128)], 7, j * 128)
    cross_count = len(copies)
    for i in range(2):
        put(r.ffn_in.at[:, pl.ds(i * 128, 128)], 8 + i)
    for i in range(2):
        for j in range(4):
            put(r.ffn_out.at[pl.ds(i * 128, 128), pl.ds(j * 128, 128)], 10 + i, j * 128)
    return copies[:self_count], copies[self_count:cross_count], copies[cross_count:]


LOADS = 24


def by_table(dst, src):
    rows = jnp.swapaxes(src[...], 0, 1)
    if len(dst.shape) == 3:
        dst[...] = rows
    else:
        for t in range(4):
            dst[pl.ds(t * MPAD, MPAD), :] = rows[t]


def table_rows(ref, t):
    return ref.at[t] if len(ref.shape) == 3 else ref.at[pl.ds(t * MPAD, MPAD)]


def layer_kernel(r):
    place = Place()
    links = Links(r.send_sems, r.recv_sems)
    greet_start(place)
    first_loads = []
    for n, (src, dst) in enumerate(
        ((r.tags, r.tags_p), (r.memory, r.mem_p.at[pl.ds(0, MLOC)]), (r.cotangent, r.cot_p))
    ):
        copy = pltpu.make_async_copy(src, dst, r.load_sems.at[LOADS - 3 + n])
        copy.start()
        first_loads.append(copy)
    loads = load_weights(r, place, r.load_sems)

    tags = Spread(place, links, r.tags_t, r.x, L // 4)
    memory = Spread(place, links, r.mem_t, r.m, MPAD)
    cotangent = Spread(place, links, r.cot_t, r.cot, L // 4)
    w_self = Gather(place, links, r.w, 0, 2)
    w_cross, w_ffn = (Gather(place, links, r.w, unit, 2) for unit in (4, 8))
    result = Collect(place, links, r.result, r.result_t)
    tags_grad = Collect(place, links, r.tgrad, r.tgrad_t)
    memory_grad = Collect(place, links, r.mgrad, r.mgrad_t)
    lens = Phase(links, r.lens)
    small_near, small_far = Phase(links, r.small.at[0]), Phase(links, r.small.at[pl.ds(0, 2)])
    def group(unit, per, landing, bufs, n, split=False):
        views = [getattr(r, name).at[n] for name in bufs]
        return Halves(place, links, r, unit, landing), Reduce(place, links, r, unit, per, views, split)

    def freed(first, unit):
        return [r.w.at[first + k, pl.ds(unit, 2)] for k in range(2)]

    one, two = ("s1", "t1", "s2", "t2", "s3"), ("r1", "b1", "r2", "b2", "r3")
    h_out, g_out = group(10, 1, [r.s0.at[k] for k in range(2)], one, 0)
    h_mid, g_mid = group(6, 2, [r.r0.at[k] for k in range(2)], two, 0)
    h_cross, g_cross = group(4, 1, freed(0, 8), one, 1)
    h_value, g_value = group(2, 1, freed(2, 8), one, 2)
    h_query, g_query = group(0, 1, freed(2, 10), one, 3, split=True)
    g_small = SmallReduce(place, links, r)
    assert links.used <= SLOTS
    out = Results(r)

    for t in range(4):
        r.lens_own[pl.ds(t, 1), :] = jnp.full((1, 128), r.tag_lengths[t], jnp.int32)
        r.lens_own[pl.ds(4 + t, 1), :] = jnp.full((1, 128), r.mem_lengths[t], jnp.int32)
    r.small[place.mp, pl.ds(0, 2), :] = r.self_qv_bias[...].astype(F32)
    r.small[place.mp, pl.ds(2, 2), :] = r.cross_qv_bias[...].astype(F32)
    r.small[place.mp, pl.ds(4, 2), :] = r.ffn_in_bias[...].astype(F32)
    r.small[place.mp, pl.ds(6, 2), :] = jnp.zeros((2, 128), F32)
    for n, part in enumerate((r.out_bias, r.norm_gain, r.norm_bias)):
        r.pvec[pl.ds(3 * n, 3), :] = part[...].astype(F32)
    first_loads[0].wait()
    by_table(r.tags_t, r.tags_p)
    greet_wait(place)
    for copy in loads[0]:
        copy.wait()
    w_self.start()
    tags.start()
    lens.send(r.lens_own, r.lens, place.device(lo=1 - place.lo))
    w_self.start_near()
    own = r.small.at[place.mp]
    small_near.send(own, own, place.sibling())
    for core in (place.core, 1 - place.core):
        small_far.send(own, own, place.device(lo=1 - place.lo, hi=1 - place.hi, core=core))
    for copy in loads[1] + loads[2]:
        copy.wait()
    r.w[place.mp, pl.ds(5, 2)] = jnp.swapaxes(r.kv_pairs[...], 0, 1)
    w_cross.start()
    w_ffn.start()
    w_self.step_first()
    first_loads[1].wait()
    r.mem_p[pl.ds(MLOC, MPAD - MLOC)] = jnp.zeros((MPAD - MLOC, 4, D), BF)
    by_table(r.mem_t, r.mem_p)
    memory.start()
    w_cross.start_near()
    w_ffn.start_near()
    w_self.step_second()
    first_loads[2].wait()
    by_table(r.cot_t, r.cot_p)
    cotangent.start()
    w_cross.step_first()
    lens.wait()
    stage_self_mask(r)

    small_near.wait()
    w_self.near.wait()
    tags.wait()
    stage_qkv(r, place.hi)
    w_self.step_last()
    w_cross.step_second()
    w_ffn.step_first()
    stage_self(r, place.hi)
    small_far.wait()
    w_self.far.wait()
    stage_qkv(r, 1 - place.hi)
    w_cross.step_last()
    w_ffn.step_second()
    stage_self(r, 1 - place.hi)
    stage_first(r)
    w_cross.near.wait()
    w_cross.far.wait()
    stage_cross_mask(r)
    stage_cross_q(r)
    memory.wait()
    stage_cross_kv(r)
    w_ffn.step_last()
    stage_cross(r)
    w_ffn.near.wait()
    w_ffn.far.wait()
    kept = stage_rows(r, cotangent.wait)
    links.finish()
    result.start()
    stage_ffn_out_grads(r)
    h_out.start(0)
    h_out.start(1)
    stage_rows_back(r, kept)
    h_out.add(g_out, 0)
    h_out.add(g_out, 1)
    g_out.step_plane()
    stage_ffn_grads(r)
    stage_cross_out_grad(r)
    stage_cross_values(r)
    stage_cross_value_grads(r)
    h_mid.start(0)
    h_mid.start(1)
    g_out.step_line()
    stage_cross_back(r, 0)
    h_mid.add(g_mid, 0)
    h_mid.add(g_mid, 1)
    g_mid.step_plane()
    g_out.step_z()
    stage_cross_back(r, 1)
    g_out.step_spread()
    stage_memory_grad(r)
    memory_grad.start()
    stage_cross_grads(r)
    h_cross.start(0)
    h_cross.start(1)
    g_out.step_spread_more()
    stage_first_back(r)
    h_cross.add(g_cross, 0)
    h_cross.add(g_cross, 1)
    g_cross.step_plane()
    stage_self_out_grad(r)
    stage_self_values(r)
    h_value.start(0)
    h_value.start(1)
    g_mid.step_line()
    stage_self_back(r, 0)
    h_value.add(g_value, 0)
    h_value.add(g_value, 1)
    g_value.step_plane()
    stage_self_grads(r, 0)
    h_query.start(0)
    stage_self_back(r, 1)
    h_query.add(g_query, 0)
    g_query.step_plane(0)
    g_mid.step_z()
    g_cross.step_line()
    stage_self_grads(r, 1)
    h_query.start(1)
    g_small.start()
    stage_tags_grad(r)
    tags_grad.start()
    h_query.add(g_query, 1)
    g_query.step_plane(1)
    g_small.step_x()
    g_mid.step_spread()
    g_cross.step_z()
    g_value.step_line()
    g_out.wait()
    out.units(10, 2)
    result.wait()
    out.rows(r.result_t, r.tags_p, r.result_out)
    g_small.step_y()
    g_query.step_line()
    g_cross.step_spread()
    g_value.step_z()
    g_mid.step_spread_more()
    g_small.step_z()
    memory_grad.wait()
    out.rows(r.mgrad_t, r.mem_p, r.mgrad_out, MLOC)
    g_query.step_z()
    g_value.step_spread()
    g_cross.step_spread_more()
    g_small.wait()
    g_query.step_spread()
    g_value.step_spread_more()
    g_mid.wait()
    out.units(6, 4)
    g_query.step_spread_more()
    g_cross.wait()
    out.units(4, 2)
    tags_grad.wait()
    out.rows(r.tgrad_t, r.cot_p, r.tgrad_out)
    g_value.wait()
    out.units(2, 2)
    g_query.wait()
    out.units(0, 2)
    out.finish()
    links.finish()


def deliver(arrays, outs):
    plain = [name for name in outs if name in arrays]
    made = [name for name in outs if name not in arrays]
    names = plain + ["fin_out"]

    def kernel(*refs):
        refs = list(refs)
        sems = refs.pop()
        srcs = dict(zip(names, refs))
        dsts = dict(zip(outs, refs[len(names) :]))
        held = dict(zip(names + made, refs[len(names) + len(outs) :]))
        reads = {}
        for n, name in enumerate(plain):
            reads[name] = pltpu.make_async_copy(srcs[name], held[name], sems.at[0, n])
            reads[name].start()
        fin = held["fin_out"]
        for n in range(3):
            span = pl.ds(4 * n, 4)
            reads[n] = pltpu.make_async_copy(srcs["fin_out"].at[span], fin.at[span], sems.at[0, len(plain) + n])
            reads[n].start()
        writes = []

        def write(name):
            copy = pltpu.make_async_copy(held[name], dsts[name], sems.at[1, len(writes)])
            copy.start()
            writes.append(copy)

        def blocks(name, first, unit):
            for j in range(4):
                part = fin[unit, pl.ds(j * 128, 128), :].astype(F32)
                held[name][pl.ds(first, 128), pl.ds(j * 128, 128)] = part

        for name in plain:
            reads[name].wait()
            write(name)
        reads[0].wait()
        for j in range(3):
            held["gself_qkv_out"][j] = fin[j].astype(F32)
        write("gself_qkv_out")
        blocks("gself_out_out", 0, 3)
        write("gself_out_out")
        reads[1].wait()
        held["gcross_q_out"][...] = fin[4].astype(F32)
        write("gcross_q_out")
        held["gcross_kv_out"][...] = jnp.swapaxes(fin[pl.ds(5, 2)].astype(F32), 0, 1)
        write("gcross_kv_out")
        blocks("gcross_out_out", 0, 7)
        write("gcross_out_out")
        reads[2].wait()
        for i in range(2):
            held["gffn_in_out"][:, pl.ds(i * 128, 128)] = fin[8 + i].astype(F32)
        write("gffn_in_out")
        for i in range(2):
            blocks("gffn_out_out", i * 128, 10 + i)
        write("gffn_out_out")
        for copy in writes:
            copy.wait()

    hbm = pl.BlockSpec(memory_space=pltpu.HBM)
    shapes = [arrays[name] for name in names] + [outs[name] for name in made]
    return pl.pallas_call(
        kernel,
        out_shape=tuple(outs.values()),
        in_specs=[hbm] * len(names),
        out_specs=(hbm,) * len(outs),
        scratch_shapes=[pltpu.VMEM(a.shape, a.dtype) for a in shapes] + [pltpu.SemaphoreType.DMA((2, len(outs)))],
        compiler_params=pltpu.CompilerParams(vmem_limit_bytes=62 * 1024 * 1024),
        name="deliver",
    )(*[arrays[name] for name in names])


SLOTS = 80


def per_device(
    tags,
    memory,
    cotangent,
    tag_lengths,
    mem_lengths,
    self_qkv,
    self_qv_bias,
    self_out,
    cross_q,
    cross_kv,
    cross_qv_bias,
    cross_out,
    ffn_in,
    ffn_in_bias,
    ffn_out,
    out_bias,
    norm_gain,
    norm_bias,
):
    ins = dict(
        tags=tags,
        memory=memory,
        cotangent=cotangent,
        tag_lengths=tag_lengths,
        mem_lengths=mem_lengths,
        self_qkv=jnp.transpose(self_qkv, (1, 0, 2)),
        self_qv_bias=self_qv_bias,
        self_out=self_out,
        cross_q=cross_q,
        cross_kv=cross_kv,
        cross_qv_bias=cross_qv_bias,
        cross_out=cross_out,
        ffn_in=ffn_in,
        ffn_in_bias=ffn_in_bias.reshape(2, 128),
        ffn_out=ffn_out,
        out_bias=out_bias,
        norm_gain=norm_gain,
        norm_bias=norm_bias,
    )
    in_smem = ("tag_lengths", "mem_lengths")
    in_vmem = ("self_qv_bias", "cross_qv_bias", "ffn_in_bias", "out_bias", "norm_gain", "norm_bias")

    def shape(*dims, dtype=F32):
        return jax.ShapeDtypeStruct(dims, dtype)

    outs = dict(
        result_out=shape(L // 4, 4, D, dtype=BF),
        tgrad_out=shape(L // 4, 4, D, dtype=BF),
        mgrad_out=shape(MLOC, 4, D, dtype=BF),
        gself_qkv_out=shape(3, D, 128),
        gself_qv=shape(2, 128),
        gself_out_out=shape(128, D),
        gcross_q_out=shape(D, 128),
        gcross_kv_out=shape(D, 2, 128),
        gcross_qv=shape(2, 128),
        gcross_out_out=shape(128, D),
        gffn_in_out=shape(D, 256),
        gffn_bias=shape(2, 128),
        gffn_out_out=shape(256, D),
        gout_bias=shape(3, 128),
        gnorm_gain=shape(3, 128),
        gnorm_bias=shape(3, 128),
    )
    own_outs = {name: outs[name] for name in ("result_out", "tgrad_out", "mgrad_out") + SMALL_OUTS}
    own_outs["fin_out"] = shape(12, D, 128, dtype=BF)
    vm = pltpu.VMEM
    scratch = scratch_list()
    scratch.update(
        x=vm((L, D), BF), m=vm((MT, D), BF), cot=vm((L, D), BF),
        lens=vm((8, 128), jnp.int32), lens_own=vm((8, 128), jnp.int32),
        w=vm((4, 12, D, 128), BF), small=vm((4, 8, 128), F32), pvec=vm((16, D), F32),
        tags_p=vm((L // 4, 4, D), BF), mem_p=vm((MPAD, 4, D), BF), cot_p=vm((L // 4, 4, D), BF),
        result=vm((4, L // 4, D), BF), tags_t=vm((4, L // 4, D), BF), mem_t=vm((MT, D), BF), cot_t=vm((4, L // 4, D), BF),
        result_t=vm((4, L // 4, D), BF), mgrad_t=vm((4, MPAD, D), BF), tgrad_t=vm((4, L // 4, D), BF),
        kv_pairs=vm((D, 2, 128), BF), fin=vm((12, D, 128), BF),
        grads=vm((2, 2, 12, D, 128), BF), sums=vm((16, D), F32), bsums=vm((4, 8, 128), F32),
        r0=vm((2, 4, D, 128), BF),
        r1=vm((1, 2, 3, 2, 2, 128, 128), BF), b1=vm((1, 2, 2, 2, 128, 128), BF),
        r2=vm((1, 2, 3, 2, 2, 32, 128), BF), b2=vm((1, 2, 2, 2, 32, 128), BF), r3=vm((1, 3, 2, 2, 32, 128), BF),
        s0=vm((2, 2, D, 128), BF), s1=vm((4, 2, 3, 2, 1, 128, 128), BF), t1=vm((4, 2, 2, 1, 128, 128), BF),
        s2=vm((4, 2, 3, 2, 1, 32, 128), BF), t2=vm((4, 2, 2, 1, 32, 128), BF), s3=vm((4, 3, 2, 1, 32, 128), BF),
        sm=vm((2, 2, 16, 128), F32), sm0=vm((2, 16, 128), F32),
        smx=vm((4, 2, 16, 128), F32), smy=vm((4, 2, 16, 128), F32), smz=vm((4, 2, 16, 128), F32),
        send_sems=pltpu.SemaphoreType.DMA((SLOTS,)),
        recv_sems=pltpu.SemaphoreType.DMA((SLOTS,)),
        load_sems=pltpu.SemaphoreType.DMA((LOADS,)),
        out_sems=pltpu.SemaphoreType.DMA((16,)),
    )
    names = tuple(ins) + tuple(own_outs) + tuple(scratch)
    anywhere = pl.BlockSpec(memory_space=pl.ANY)
    on_chip = pl.BlockSpec(memory_space=pltpu.VMEM)

    def kernel(*refs):
        layer_kernel(Refs(**dict(zip(names, refs))))

    def space(name):
        if name in in_smem:
            return pl.BlockSpec(memory_space=pltpu.SMEM)
        return on_chip if name in in_vmem + SMALL_OUTS else anywhere

    results = pl.pallas_call(
        kernel,
        out_shape=tuple(own_outs.values()),
        in_specs=[space(name) for name in ins],
        out_specs=tuple(space(name) for name in own_outs),
        scratch_shapes=list(scratch.values()),
        compiler_params=pltpu.CompilerParams(
            vmem_limit_bytes=62 * 1024 * 1024, collective_id=0, has_side_effects=True
        ),
        name="layer",
    )(*ins.values())
    results = deliver(dict(zip(own_outs, results)), outs)
    results = dict(zip(outs, results))
    results["gself_qkv_out"] = jnp.transpose(results["gself_qkv_out"], (1, 0, 2))
    results["gffn_bias"] = results["gffn_bias"].reshape(256)
    return tuple(results.values())


def solution(mesh):
    return jax.shard_map(
        per_device,
        mesh=mesh,
        in_specs=(
            P("mp", "dp", None),
            P("mp", "dp", None),
            P("mp", "dp", None),
            P("dp"),
            P("dp"),
            P(None, None, "mp"),
            P(None, "mp"),
            P("mp", None),
            P(None, "mp"),
            P(None, None, "mp"),
            P(None, "mp"),
            P("mp", None),
            P(None, "mp"),
            P("mp"),
            P("mp", None),
            P(),
            P(),
            P(),
        ),
        out_specs=(
            P("mp", "dp", None),
            P("mp", "dp", None),
            P("mp", "dp", None),
            P(None, None, "mp"),
            P(None, "mp"),
            P("mp", None),
            P(None, "mp"),
            P(None, None, "mp"),
            P(None, "mp"),
            P("mp", None),
            P(None, "mp"),
            P("mp"),
            P("mp", None),
            P(None, "mp"),
            P(None, "mp"),
            P(None, "mp"),
        ),
        check_vma=False,
    )
```

```python
import math

import jax
import jax.numpy as jnp
from jax import lax
from jax.experimental import pallas as pl
from jax.experimental.pallas import tpu as pltpu
from jax.sharding import PartitionSpec as P

BF = jnp.bfloat16
F32 = jnp.float32
D = 512
HEADS = 4
HEAD = 128
L = 512
MLOC = 196
MPAD = 208
MT = 4 * MPAD
QB = 256
EPSILON = 1e-05
SCALE = 1.0 / math.sqrt(HEAD)
LOG2E = math.log2(math.e)
NEG = -1e30


def mm(a, b):
    return jnp.dot(a, b, preferred_element_type=F32)


def mm_nt(a, b):
    return lax.dot_general(a, b, (((1,), (1,)), ((), ())), preferred_element_type=F32)


def mm_tn(a, b):
    return lax.dot_general(a, b, (((0,), (0,)), ((), ())), preferred_element_type=F32)


def col_weight(w, unit):
    return jnp.concatenate([w[s, unit] for s in range(4)], axis=1)


def row_block(w, s, unit):
    return jnp.concatenate([w[s, unit, pl.ds(j * 128, 128), :] for j in range(4)], axis=1)


def row_weight(w, unit):
    return jnp.concatenate([row_block(w, s, unit) for s in range(4)], axis=0)


def put_cols(g, unit, value):
    for s in range(4):
        g[s // 2, s % 2, unit] = value[:, s * 128 : (s + 1) * 128].astype(BF)


def put_rows(g, s, unit, value):
    for j in range(4):
        g[s // 2, s % 2, unit, pl.ds(j * 128, 128), :] = value[:, j * 128 : (j + 1) * 128].astype(BF)


def norm_rows(v):
    center = v - jnp.mean(v, axis=-1, keepdims=True)
    inverse = lax.rsqrt(jnp.mean(center * center, axis=-1, keepdims=True) + EPSILON)
    return center * inverse, inverse


def norm_back(e, unit, inverse, gain):
    scaled = e * gain
    return inverse * (
        scaled
        - jnp.mean(scaled, axis=-1, keepdims=True)
        - unit * jnp.mean(scaled * unit, axis=-1, keepdims=True)
    )


def norm_back_rows(r, n, e, unit, inverse):
    gain = r.pvec[pl.ds(3 + n, 1), :]
    totals = [jnp.zeros((8, D), F32)] * 3
    for i in range(L // 128):
        rows = slice(i * 128, (i + 1) * 128)
        ei, ui = e[rows, :].astype(F32), unit[rows, :]
        di = norm_back(ei, ui, inverse[rows, :], gain)
        yield rows, di
        parts = (di, ei * ui, ei)
        totals = [t + jnp.sum(v.reshape(16, 8, D), axis=0) for t, v in zip(totals, parts)]
    for j in range(3):
        r.sums[pl.ds(3 * j + n, 1), :] = jnp.sum(totals[j], axis=0, keepdims=True)


GELU_C = math.sqrt(2.0 / math.pi)


def gelu_both(z):
    z2 = z * z
    t = jnp.tanh(GELU_C * z * (1.0 + 0.044715 * z2))
    half = 0.5 * (1.0 + t)
    return z * half, half + (0.5 * GELU_C) * z * (1.0 - t * t) * (1.0 + 3 * 0.044715 * z2)


def col_sum(v):
    return jnp.sum(v, axis=0, keepdims=True)


def bias_row(small, row):
    return jnp.concatenate([small[s, pl.ds(row, 1), :] for s in range(4)], axis=1)


def head_rows(h):
    return pl.ds(h * HEAD if isinstance(h, int) else pl.multiple_of(h * HEAD, HEAD), HEAD)


def attend(q, k, v, p, ot, rinv, sbuf, keybias, causal, limit, key_block, heads):
    items = [(h, qb) for h in heads for qb in range(L // QB)]
    peaks, totals = {}, {}

    def score(i, kb):
        h, qb = items[i]
        rows = pl.ds(kb * key_block, key_block)
        s = mm_nt(k[h, rows, :], q[h, pl.ds(qb * QB, QB), :])
        s = s + jnp.concatenate([keybias[rows, :]] * (QB // 128), axis=1)
        if causal and kb == qb:
            key = lax.broadcasted_iota(jnp.int32, s.shape, 0)
            query = lax.broadcasted_iota(jnp.int32, s.shape, 1)
            s = jnp.where(key <= query, s, NEG)
        sbuf[i % 2, rows, :] = s
        top = jnp.max(s, axis=0, keepdims=True)
        peaks[i] = jnp.maximum(peaks[i], top) if kb else top

    def weigh(i, kb):
        h, qb = items[i]
        rows = pl.ds(kb * key_block, key_block)
        e = jnp.exp2(sbuf[i % 2, rows, :] * (SCALE * LOG2E) - peaks[i] * (SCALE * LOG2E))
        p[h, rows, pl.ds(qb * QB, QB)] = e.astype(BF)
        part = jnp.sum(e, axis=0, keepdims=True)
        totals[i] = totals[i] + part if kb else part

    def output(i):
        h, qb = items[i]
        cols, keys = pl.ds(qb * QB, QB), limit(qb)
        inv = 1.0 / totals[i]
        rinv[h, :, cols] = jnp.broadcast_to(inv, (8, QB))
        o = mm(v[h, pl.ds(0, keys), :].T, p[h, pl.ds(0, keys), cols])
        ot[head_rows(h), cols] = (o * inv).astype(BF)

    blocks = [limit(qb) // key_block for _, qb in items]
    for i in range(len(items) + 2):
        ahead = blocks[i] if i < len(items) else 0
        behind = blocks[i - 1] if 0 < i <= len(items) else 0
        for kb in range(max(ahead, behind)):
            if kb < ahead:
                score(i, kb)
            if kb < behind:
                weigh(i - 1, kb)
        if i > 1:
            output(i - 2)


def scaled_heads(do, grad, rinv):
    for h in range(HEADS):
        inv = rinv[h].T[:, :1]
        do[h] = (grad[:, h * HEAD : (h + 1) * HEAD] * inv).astype(BF)


def attend_grad(q, k, v, p, ot, do, dqt, dk, dsbuf, limit, key_block, pair):
    def one(h):
        kt = k[h].T
        span = head_rows(h)
        delta = jnp.sum(ot[span, :].astype(F32) * do[h].T.astype(F32), axis=0, keepdims=True)
        for qb in range(L // QB):
            cols = pl.ds(qb * QB, QB)
            keys = limit(qb)
            dov = do[h, cols, :]
            low = delta[:, qb * QB : (qb + 1) * QB]
            for kb in range(keys // key_block):
                rows = pl.ds(kb * key_block, key_block)
                dw = mm_nt(v[h, rows, :], dov)
                dsbuf[rows, cols] = (p[h, rows, cols].astype(F32) * (dw - low)).astype(BF)
            dq = mm(kt[:, :keys], dsbuf[pl.ds(0, keys), cols]) * SCALE
            dqt[span, cols] = dq.astype(BF)
        for rows, seen in seen_blocks(limit):
            dk[h, rows, :] = (mm(dsbuf[rows, seen], q[h, seen, :]) * SCALE).astype(BF)

    one(2 * pair)
    one(2 * pair + 1)


def seen_blocks(limit):
    below = 0
    for qb in range(L // QB):
        keys = limit(qb) - below
        if keys:
            yield pl.ds(below, keys), pl.ds(qb * QB, L - qb * QB)
        below = limit(qb)


def value_grad(p, do, dv, limit):
    def one(h):
        for rows, seen in seen_blocks(limit):
            dv[h, rows, :] = mm(p[h, rows, seen], do[h, seen, :]).astype(BF)

    for h in range(HEADS):
        one(h)


def scratch_list():
    v = pltpu.VMEM
    return dict(
        q=v((4, L, HEAD), BF), k=v((4, L, HEAD), BF), v=v((4, L, HEAD), BF),
        ps=v((4, L, L), BF), ots=v((D, L), BF), rs=v((4, 8, L), F32),
        h1=v((L, D), F32), h1b=v((L, D), BF), u1=v((L, D), F32), inv1=v((L, 1), F32),
        qc=v((4, L, HEAD), BF), kc=v((4, MT, HEAD), BF), vc=v((4, MT, HEAD), BF),
        pc=v((4, MT, L), BF), otc=v((D, L), BF), rc=v((4, 8, L), F32),
        h2b=v((L, D), BF), g=v((L, 2 * D), BF), dfb=v((L, D), BF), dz=v((L, 2 * D), BF),
        dr2=v((L, D), F32), da2=v((L, D), BF), doc=v((4, L, HEAD), BF),
        dkc=v((4, MT, HEAD), BF), dvc=v((4, MT, HEAD), BF), dqc=v((L, D), BF),
        sbuf=v((2, MT, QB), F32), dsbuf=v((MT, L), BF), keybias=v((MT, 128), F32),
    )


class Refs:
    def __init__(self, **kw):
        self.__dict__.update(kw)
        self.ob = self.dq = self.dqc
        self.xt = self.h2b
        self.dqt, self.dr1 = self.otc, self.h1
        self.da1, self.dos = self.da2, self.doc
        self.dk, self.dv = self.qc, self.vc.at[:, pl.ds(0, L), :]
        self.tgrad, self.mgrad = self.cot_t, self.mem_t


def stage_qkv(r, pair):
    heads = (2 * pair, 2 * pair + 1)
    for j, (dst, row) in enumerate(((r.q, 0), (r.k, None), (r.v, 1))):
        y = mm(r.x[...], jnp.concatenate([r.w[h, j] for h in heads], axis=1))
        if row is not None:
            y = y + jnp.concatenate([r.small[h, pl.ds(row, 1), :] for h in heads], axis=1)
        y = y.astype(BF)
        for i, h in enumerate(heads):
            dst[h] = y[:, i * HEAD : (i + 1) * HEAD]


def self_limit(qb):
    return (qb + 1) * QB


def stage_self_mask(r):
    key = lax.broadcasted_iota(jnp.int32, (L, 128), 0)
    r.keybias[pl.ds(0, L), :] = jnp.where(key < r.lens[pl.ds(lax.axis_index("mp"), 1), :], 0.0, NEG)


def stage_cross_mask(r):
    token = lax.broadcasted_iota(jnp.int32, (MPAD, 128), 0)
    memlen = r.lens[pl.ds(4 + lax.axis_index("mp"), 1), :]
    for i in range(4):
        seen = (token < MLOC) & (token + i * MLOC < memlen)
        r.keybias[pl.ds(i * MPAD, MPAD), :] = jnp.where(seen, 0.0, NEG)


def stage_self(r, pair):
    heads = (2 * pair, 2 * pair + 1)
    attend(r.q, r.k, r.v, r.ps, r.ots, r.rs, r.sbuf, r.keybias, True, self_limit, QB, heads)


def stage_first(r):
    r.ob[...] = r.ots[...].T
    wso = row_weight(r.w, 3)

    rows = pl.ds(0, L)
    v = r.x[rows, :].astype(F32) + mm(r.ob[rows, :], wso) + r.pvec[pl.ds(0, 1), :]
    unit, inv = norm_rows(v)
    r.u1[rows, :] = unit
    r.inv1[rows, :] = inv
    h1 = unit * r.pvec[pl.ds(3, 1), :] + r.pvec[pl.ds(6, 1), :]
    r.h1[rows, :] = h1
    r.h1b[rows, :] = h1.astype(BF)


def stage_cross_q(r):
    y = (mm(r.h1b[...], col_weight(r.w, 4)) + bias_row(r.small, 2)).astype(BF)
    for h in range(HEADS):
        r.qc[h] = y[:, h * HEAD : (h + 1) * HEAD]


def stage_cross_kv(r):
    for j, (dst, row) in enumerate(((r.kc, None), (r.vc, 3))):
        y = mm(r.m[...], col_weight(r.w, 5 + j))
        if row is not None:
            y = y + bias_row(r.small, row)
        y = y.astype(BF)
        for h in range(HEADS):
            dst[h] = y[:, h * HEAD : (h + 1) * HEAD]


def cross_limit(qb):
    return MT


def stage_cross(r):
    attend(r.qc, r.kc, r.vc, r.pc, r.otc, r.rc, r.sbuf, r.keybias, False, cross_limit, MPAD, range(HEADS))


def ffn_weights(r, s):
    w_in = jnp.concatenate([r.w[s, 8], r.w[s, 9]], axis=1)
    w_out = jnp.concatenate([row_block(r.w, s, 10), row_block(r.w, s, 11)], axis=0)
    return w_in, w_out


def stage_rows(r, cotangent_ready=lambda: None):
    r.ob[...] = r.otc[...].T

    v = r.h1[...] + mm(r.ob[...], row_weight(r.w, 7)) + r.pvec[pl.ds(1, 1), :]
    u2, inv2 = norm_rows(v)
    h2 = u2 * r.pvec[pl.ds(4, 1), :] + r.pvec[pl.ds(7, 1), :]
    h2b = h2.astype(BF)
    r.h2b[...] = h2b
    r3 = h2 + r.pvec[pl.ds(2, 1), :]
    slopes = []
    for s in range(4):
        w_in, w_out = ffn_weights(r, s)
        bias = jnp.concatenate([r.small[s, pl.ds(4, 1), :], r.small[s, pl.ds(5, 1), :]], axis=1)
        value, slope = gelu_both(mm(h2b, w_in) + bias)
        value = value.astype(BF)
        r.g[:, pl.ds(s * 256, 256)] = value
        slopes.append(slope)
        r3 = r3 + mm(value, w_out)
    u3, inv3 = norm_rows(r3)
    value = (u3 * r.pvec[pl.ds(5, 1), :] + r.pvec[pl.ds(8, 1), :]).astype(BF)
    for i in range(4):
        r.result[i] = value[i * 128 : (i + 1) * 128, :]
    cotangent_ready()
    r.dr2[...] = u2
    for rows, dr3 in norm_back_rows(r, 2, r.cot, u3, inv3):
        r.dr1[rows, :] = dr3
        r.dfb[rows, :] = dr3.astype(BF)
    return inv2, slopes


def stage_rows_back(r, kept):
    inv2, slopes = kept
    e2 = r.dr1[...]
    for s in range(4):
        w_in, w_out = ffn_weights(r, s)
        dz = (mm_nt(r.dfb[...], w_out) * slopes[s]).astype(BF)
        r.dz[:, pl.ds(s * 256, 256)] = dz
        e2 = e2 + mm_nt(dz, w_in)
    for rows, dr2 in norm_back_rows(r, 1, e2, r.dr2, inv2):
        r.dr2[rows, :] = dr2
        r.da2[rows, :] = dr2.astype(BF)
    scaled_heads(r.doc, mm_nt(r.da2[...], row_weight(r.w, 7)), r.rc)


def stage_ffn_out_grads(r):
    gt = r.g[...].T
    for s in range(4):
        y = mm(gt[s * 256 : (s + 1) * 256, :], r.dfb[...])
        for i in range(2):
            put_rows(r.grads, s, 10 + i, y[i * 128 : (i + 1) * 128, :])


def stage_ffn_grads(r):
    h2t = r.h2b[...].T
    for s in range(4):
        y = mm(h2t, r.dz[:, pl.ds(s * 256, 256)])
        r.grads[s // 2, s % 2, 8] = y[:, :128].astype(BF)
        r.grads[s // 2, s % 2, 9] = y[:, 128:].astype(BF)
        b = col_sum(r.dz[:, pl.ds(s * 256, 256)].astype(F32))
        r.bsums[s, pl.ds(4, 1), :] = b[:, :128]
        r.bsums[s, pl.ds(5, 1), :] = b[:, 128:]


def stage_cross_out_grad(r):
    y = mm(r.otc[...], r.da2[...])
    for s in range(4):
        put_rows(r.grads, s, 7, y[s * 128 : (s + 1) * 128, :])


def stage_cross_values(r):
    value_grad(r.pc, r.doc, r.dvc, cross_limit)


def stage_cross_back(r, pair):
    attend_grad(r.qc, r.kc, r.vc, r.pc, r.otc, r.doc, r.dqt, r.dkc, r.dsbuf, cross_limit, MPAD, pair)


def stage_cross_value_grads(r):
    mt = r.m[...].T
    dv = jnp.concatenate([r.dvc[h] for h in range(HEADS)], axis=1)
    put_cols(r.grads, 6, mm(mt, dv))
    b = col_sum(dv.astype(F32))
    for h in range(HEADS):
        r.bsums[h, pl.ds(3, 1), :] = b[:, h * HEAD : (h + 1) * HEAD]


def stage_cross_grads(r):
    mt = r.m[...].T
    r.dqc[...] = r.dqt[...].T
    put_cols(r.grads, 4, mm(r.h1b[...].T, r.dqc[...]))
    put_cols(r.grads, 5, mm(mt, jnp.concatenate([r.dkc[h] for h in range(HEADS)], axis=1)))
    b = col_sum(r.dqc[...].astype(F32))
    for h in range(HEADS):
        r.bsums[h, pl.ds(2, 1), :] = b[:, h * HEAD : (h + 1) * HEAD]


def stage_memory_grad(r):
    w = jnp.concatenate([col_weight(r.w, 5), col_weight(r.w, 6)], axis=1)
    parts = [d[h] for d in (r.dkc, r.dvc) for h in range(HEADS)]
    r.mgrad[...] = mm_nt(jnp.concatenate(parts, axis=1), w).astype(BF)


def stage_first_back(r):
    e1 = r.dr2[...] + mm_nt(r.dqc[...], col_weight(r.w, 4))
    for rows, dr1 in norm_back_rows(r, 0, e1, r.u1, r.inv1):
        r.dr1[rows, :] = dr1
        r.da1[rows, :] = dr1.astype(BF)
    scaled_heads(r.dos, mm_nt(r.da1[...], row_weight(r.w, 3)), r.rs)


def stage_self_out_grad(r):
    y = mm(r.ots[...], r.da1[...])
    for s in range(4):
        put_rows(r.grads, s, 3, y[s * 128 : (s + 1) * 128, :])


def stage_self_back(r, pair):
    attend_grad(r.q, r.k, r.v, r.ps, r.ots, r.dos, r.dqt, r.dk, r.dsbuf, self_limit, QB, pair)


def stage_self_values(r):
    value_grad(r.ps, r.dos, r.dv, self_limit)
    r.xt[...] = r.x[...].T
    dv = jnp.concatenate([r.dv[h] for h in range(HEADS)], axis=1)
    put_cols(r.grads, 2, mm(r.xt[...], dv))
    b = col_sum(dv.astype(F32))
    for h in range(HEADS):
        r.bsums[h, pl.ds(1, 1), :] = b[:, h * HEAD : (h + 1) * HEAD]


def stage_self_grads(r, pair):
    cols = pl.ds(pair * 256, 256)
    dq = r.dqt[cols, :].T
    r.dq[:, cols] = dq
    y = mm(r.xt[...], jnp.concatenate([dq, r.dk[2 * pair], r.dk[2 * pair + 1]], axis=1))
    b = col_sum(dq.astype(F32))
    for i in range(2):
        for j in range(2):
            r.grads[pair, i, j] = y[:, j * 256 + i * 128 : j * 256 + (i + 1) * 128].astype(BF)
        r.bsums[2 * pair + i, pl.ds(0, 1), :] = b[:, i * 128 : (i + 1) * 128]


def stage_tags_grad(r):
    w = jnp.concatenate([col_weight(r.w, j) for j in range(3)], axis=1)
    parts = [r.dq[...]] + [d[h] for d in (r.dk, r.dv) for h in range(HEADS)]
    y = (r.dr1[...] + mm_nt(jnp.concatenate(parts, axis=1), w)).astype(BF)
    for i in range(4):
        r.tgrad[i] = y[i * 128 : (i + 1) * 128, :]


MESH = pl.DeviceIdType.MESH


class Place:
    def __init__(self):
        dp, mp = lax.axis_index("dp"), lax.axis_index("mp")
        self.mp = mp
        self.x = lax.rem(dp, 4)
        self.lo = lax.rem(lax.div(dp, 4), 2)
        self.y = lax.div(dp, 8)
        self.hi = lax.div(mp, 2)
        self.core = lax.rem(mp, 2)

    def device(self, x=None, y=None, lo=None, hi=None, core=None):
        x = self.x if x is None else x
        y = self.y if y is None else y
        lo = self.lo if lo is None else lo
        hi = self.hi if hi is None else hi
        core = self.core if core is None else core
        return (y * 8 + lo * 4 + x, hi * 2 + core)

    def owner(self, t):
        return self.device(lo=1 - self.lo, hi=t // 2, core=t % 2)

    def sibling(self):
        return self.device(core=1 - self.core)

    def across(self):
        return self.device(lo=1 - self.lo, hi=1 - self.hi)

    def x_at(self, n):
        return lax.rem(self.x + n, 4)

    def y_at(self, n):
        return lax.rem(self.y + n, 4)

    def along(self, axis, n):
        return self.device(x=self.x_at(n)) if axis == 0 else self.device(y=self.y_at(n))

    def at(self, axis, n=0):
        return self.x_at(n) if axis == 0 else self.y_at(n)

    def peers(self):
        out = [self.owner(t) for t in range(4)]
        out.append(self.sibling())
        out.append(self.device(hi=1 - self.hi))
        for axis in range(2):
            out += [self.along(axis, n) for n in (1, 2, 3)]
        return out


class Phase:
    def __init__(self, links, view):
        self.links, self.view, self.slot, self.device = links, view, links.used, None
        links.used += 1

    def send(self, src, dst, device):
        self.device = device
        pltpu.make_async_remote_copy(
            src_ref=src,
            dst_ref=dst,
            send_sem=self.links.send_sems.at[self.slot],
            recv_sem=self.links.recv_sems.at[self.slot],
            device_id=device,
            device_id_type=MESH,
        ).start()
        if self not in self.links.started:
            self.links.started.append(self)

    def whole(self):
        return pltpu.make_async_remote_copy(
            src_ref=self.view,
            dst_ref=self.view,
            send_sem=self.links.send_sems.at[self.slot],
            recv_sem=self.links.recv_sems.at[self.slot],
            device_id=self.device,
            device_id_type=MESH,
        )

    def wait(self):
        self.whole().wait_recv()

class Links:
    def __init__(self, send_sems, recv_sems):
        self.send_sems, self.recv_sems = send_sems, recv_sems
        self.used = 0
        self.started = []

    def finish(self):
        for phase in self.started:
            phase.whole().wait_send()
        self.started = []


def greet_start(place):
    barrier = pltpu.get_barrier_semaphore()
    for peer in place.peers():
        pl.semaphore_signal(barrier, inc=1, device_id=peer, device_id_type=MESH)


def greet_wait(place):
    pl.semaphore_wait(pltpu.get_barrier_semaphore(), len(place.peers()))


class Spread:
    def __init__(self, place, links, src, dst, rows):
        self.place, self.src, self.dst, self.rows = place, src, dst, rows
        self.phase = Phase(links, dst)

    def start(self):
        p = self.place
        span = pl.ds(pl.multiple_of(p.mp * self.rows, 16), self.rows)
        for t in range(4):
            self.phase.send(table_rows(self.src, t), self.dst.at[span], p.owner(t))

    def wait(self):
        self.phase.wait()


class Collect:
    def __init__(self, place, links, src, dst):
        self.place, self.src, self.dst = place, src, dst
        self.phase = Phase(links, dst)

    def start(self):
        p = self.place
        for s in range(4):
            self.phase.send(table_rows(self.src, s), self.dst.at[p.mp], p.owner(s))

    def wait(self):
        self.phase.wait()


class Gather:
    def __init__(self, place, links, w, unit, per):
        self.place, self.w, self.unit, self.per = place, w, unit, per
        some = w.at[0]
        self.z = Phase(links, some.at[pl.ds(0, 2 * per), pl.ds(0, 32)])
        self.first = Phase(links, some.at[pl.ds(0, 2 * per), pl.ds(0, 96)])
        self.second = Phase(links, some.at[pl.ds(0, 2 * per), pl.ds(0, 384)])
        self.near, self.far = (Phase(links, some.at[pl.ds(0, 2 * per)]) for _ in range(2))

    def piece(self, shard, half, rows, count):
        units = pl.ds(self.unit + self.per * half, self.per)
        return self.w.at[shard, units, pl.ds(pl.multiple_of(rows, 32), count), :]

    def other(self):
        return (1 - self.place.hi) * 2 + self.place.core

    def row(self, half):
        p = self.place
        return p.at(1 - half) * 128 + p.at(half) * 32

    def start(self):
        p = self.place
        for half in range(2):
            view = self.piece(p.mp, half, self.row(half), 32)
            self.z.send(view, view, p.across())

    def start_near(self):
        p = self.place
        whole = self.w.at[p.mp, pl.ds(self.unit, 2 * self.per)]
        self.near.send(whole, whole, p.sibling())

    def step_first(self):
        p = self.place
        self.z.wait()
        for half in range(2):
            view = self.piece(self.other(), half, self.row(half), 32)
            for n in (1, 2, 3):
                self.first.send(view, view, p.along(half, n))

    def step_second(self):
        p = self.place
        self.first.wait()
        for half in range(2):
            view = self.piece(self.other(), half, p.at(1 - half) * 128, 128)
            for n in (1, 2, 3):
                self.second.send(view, view, p.along(1 - half, n))

    def step_last(self):
        self.second.wait()
        view = self.w.at[self.other(), pl.ds(self.unit, 2 * self.per)]
        self.far.send(view, view, self.place.sibling())


class Reduce:
    def __init__(self, place, links, r, unit, per, slots, split):
        self.place, self.r, self.unit, self.per = place, r, unit, per
        self.r1, self.b1, self.r2, self.b2, self.r3 = slots
        self.split = split
        one = r.grads.at[0, 0]
        if split:
            self.plane = [Phase(links, one.at[pl.ds(0, 2 * per), pl.ds(0, 384)]) for _ in range(2)]
        else:
            self.plane = [Phase(links, self.r1)]
        self.line, self.z = Phase(links, self.r2), Phase(links, self.r3)
        self.gather = Phase(links, one.at[pl.ds(0, 2 * per), pl.ds(0, 96)])
        self.gather_more = Phase(links, one.at[pl.ds(0, 2 * per), pl.ds(0, 384)])

    def add(self, k, unit, theirs, count):
        p, r = self.place, self.r

        def one(u, carry):
            mine = r.grads[k, p.core, unit + u].astype(F32)
            r.grads[k, p.core, unit + u] = (mine + theirs[u].astype(F32)).astype(BF)
            return carry

        lax.fori_loop(0, count, one, 0)

    def step_plane(self, k=None):
        p, r = self.place, self.r
        for half in range(2):
            units = pl.ds(self.unit + self.per * half, self.per)
            for n in (1, 2, 3):
                rows = pl.ds(pl.multiple_of(p.at(half, n) * 128, 128), 128)
                if self.split:
                    src, dst = r.grads.at[k, p.core, units, rows, :], self.r1.at[half, n - 1, k]
                else:
                    src, dst = r.grads.at[:, p.core, units, rows, :], self.r1.at[half, n - 1]
                self.plane[k if self.split else 0].send(src, dst, p.along(half, n))

    def step_line(self):
        p, r = self.place, self.r
        for phase in self.plane:
            phase.wait()
        for half in range(2):
            rows = pl.ds(pl.multiple_of(p.at(half) * 128, 128), 128)

            def one(i, carry):
                k, u = lax.div(i, self.per), lax.rem(i, self.per)
                total = r.grads[k, p.core, self.unit + self.per * half + u, rows, :].astype(F32)
                for n in range(3):
                    total = total + self.r1[half, n, k, u].astype(F32)
                self.b1[half, k, u] = total.astype(BF)
                return carry

            lax.fori_loop(0, 2 * self.per, one, 0)
            for n in (1, 2, 3):
                rows = pl.ds(pl.multiple_of(p.at(1 - half, n) * 32, 32), 32)
                src = self.b1.at[half, :, :, rows, :]
                self.line.send(src, self.r2.at[half, n - 1], p.along(1 - half, n))

    def step_z(self):
        p = self.place
        self.line.wait()
        for half in range(2):
            rows = pl.ds(pl.multiple_of(p.at(1 - half) * 32, 32), 32)
            for k in range(2):
                total = self.b1[half, k, :, rows, :].astype(F32)
                for n in range(3):
                    total = total + self.r2[half, n, k].astype(F32)
                self.b2[k, half] = total.astype(BF)
        to = (
            (p.device(lo=1 - p.lo), p.hi),
            (p.device(lo=1 - p.lo, hi=1 - p.hi), 1 - p.hi),
            (p.device(hi=1 - p.hi), 1 - p.hi),
        )
        for n, (device, hi) in enumerate(to):
            self.z.send(self.b2.at[hi], self.r3.at[n], device)

    def kept(self, half, rows, count):
        units = pl.ds(self.unit + self.per * half, self.per)
        return self.r.fin.at[units, pl.ds(pl.multiple_of(rows, 32), count), :]

    def step_spread(self):
        p = self.place
        self.z.wait()
        for half in range(2):
            near = self.b2[p.hi, half].astype(F32) + self.r3[0, half].astype(F32)
            far = self.r3[1, half].astype(F32) + self.r3[2, half].astype(F32)
            view = self.kept(half, p.at(half) * 128 + p.at(1 - half) * 32, 32)
            view[...] = (near + far).astype(BF)
            for n in (1, 2, 3):
                self.gather.send(view, view, p.along(1 - half, n))

    def step_spread_more(self):
        p = self.place
        self.gather.wait()
        for half in range(2):
            view = self.kept(half, p.at(half) * 128, 128)
            for n in (1, 2, 3):
                self.gather_more.send(view, view, p.along(half, n))

    def wait(self):
        self.gather_more.wait()


class Halves:
    def __init__(self, place, links, r, unit, landing):
        self.place, self.r, self.unit, self.landing = place, r, unit, landing
        self.count = landing[0].shape[0]
        self.phases = [Phase(links, view) for view in landing]

    def start(self, k):
        p = self.place
        src = self.r.grads.at[k, 1 - p.core, pl.ds(self.unit, self.count)]
        self.phases[k].send(src, self.landing[k], p.sibling())

    def add(self, reduce, k):
        self.phases[k].wait()
        reduce.add(k, self.unit, self.landing[k], self.count)


class SmallReduce:
    def __init__(self, place, links, r):
        self.place, self.r = place, r
        self.pair = Phase(links, r.sm0)
        self.phases = [Phase(links, slots.at[pl.ds(0, 3)]) for slots in (r.smx, r.smy, r.smz)]

    def start(self):
        p, r = self.place, self.r
        for s in range(4):
            r.sm[s % 2, s // 2, pl.ds(0, 9), :] = r.sums[pl.ds(0, 9), pl.ds(s * 128, 128)]
            r.sm[s % 2, s // 2, pl.ds(9, 6), :] = r.bsums[s, pl.ds(0, 6), :]
            r.sm[s % 2, s // 2, pl.ds(15, 1), :] = jnp.zeros((1, 128), F32)
        self.pair.send(r.sm.at[1 - p.core], r.sm0, p.sibling())

    def step_x(self):
        p, r = self.place, self.r
        self.pair.wait()
        r.smx[p.x] = r.sm[p.core] + r.sm0[...]
        for n in (1, 2, 3):
            self.phases[0].send(r.smx.at[p.x], r.smx.at[p.x], p.along(0, n))

    def step_y(self):
        p, r = self.place, self.r
        self.phases[0].wait()
        r.smy[p.y] = (r.smx[0] + r.smx[1]) + (r.smx[2] + r.smx[3])
        for n in (1, 2, 3):
            self.phases[1].send(r.smy.at[p.y], r.smy.at[p.y], p.along(1, n))

    def step_z(self):
        p, r = self.place, self.r
        self.phases[1].wait()
        mine = p.hi * 2 + p.lo
        r.smz[mine] = (r.smy[0] + r.smy[1]) + (r.smy[2] + r.smy[3])
        for lo, hi in ((1 - p.lo, p.hi), (1 - p.lo, 1 - p.hi), (p.lo, 1 - p.hi)):
            self.phases[2].send(r.smz.at[mine], r.smz.at[mine], p.device(lo=lo, hi=hi))

    def wait(self):
        p, z = self.place, self.r.smz
        self.phases[2].wait()
        total = (z[0, p.hi] + z[1, p.hi]) + (z[2, p.hi] + z[3, p.hi])
        first = 0
        for name in SMALL_OUTS:
            ref = getattr(self.r, name)
            count = ref.shape[0]
            ref[...] = total[first : first + count, :]
            first += count


SMALL_OUTS = ("gout_bias", "gnorm_gain", "gnorm_bias", "gself_qv", "gcross_qv", "gffn_bias")


class Results:
    def __init__(self, r):
        self.r, self.copies = r, []

    def put(self, src, dst):
        copy = pltpu.make_async_copy(src, dst, self.r.out_sems.at[len(self.copies)])
        copy.start()
        self.copies.append(copy)

    def rows(self, tables, pairs, dst, count=None):
        pairs[...] = jnp.swapaxes(tables[...], 0, 1)
        self.put(pairs if count is None else pairs.at[pl.ds(0, count)], dst)

    def units(self, first, count):
        span = pl.ds(first, count)
        self.put(self.r.fin.at[span], self.r.fin_out.at[span])

    def finish(self):
        for copy in self.copies:
            copy.wait()


def load_weights(r, place, sem):
    mp = place.mp
    copies = []

    def put(src, unit, rows=None, count=1):
        if rows is None:
            dst = r.w.at[mp, pl.ds(unit, count)] if count > 1 else r.w.at[mp, unit]
        else:
            dst = r.w.at[mp, unit, pl.ds(rows, 128), :]
        copy = pltpu.make_async_copy(src, dst, sem.at[len(copies)])
        copy.start()
        copies.append(copy)

    put(r.self_qkv, 0, count=3)
    for j in range(4):
        put(r.self_out.at[:, pl.ds(j * 128, 128)], 3, j * 128)
    self_count = len(copies)
    put(r.cross_q, 4)
    copy = pltpu.make_async_copy(r.cross_kv, r.kv_pairs, sem.at[len(copies)])
    copy.start()
    copies.append(copy)
    for j in range(4):
        put(r.cross_out.at[:, pl.ds(j * 128, 128)], 7, j * 128)
    cross_count = len(copies)
    for i in range(2):
        put(r.ffn_in.at[:, pl.ds(i * 128, 128)], 8 + i)
    for i in range(2):
        for j in range(4):
            put(r.ffn_out.at[pl.ds(i * 128, 128), pl.ds(j * 128, 128)], 10 + i, j * 128)
    return copies[:self_count], copies[self_count:cross_count], copies[cross_count:]


LOADS = 24


def by_table(dst, src):
    rows = jnp.swapaxes(src[...], 0, 1)
    if len(dst.shape) == 3:
        dst[...] = rows
    else:
        for t in range(4):
            dst[pl.ds(t * MPAD, MPAD), :] = rows[t]


def table_rows(ref, t):
    return ref.at[t] if len(ref.shape) == 3 else ref.at[pl.ds(t * MPAD, MPAD)]


def layer_kernel(r):
    place = Place()
    links = Links(r.send_sems, r.recv_sems)
    greet_start(place)
    first_loads = []
    for n, (src, dst) in enumerate(
        ((r.tags, r.tags_p), (r.memory, r.mem_p.at[pl.ds(0, MLOC)]), (r.cotangent, r.cot_p))
    ):
        copy = pltpu.make_async_copy(src, dst, r.load_sems.at[LOADS - 3 + n])
        copy.start()
        first_loads.append(copy)
    loads = load_weights(r, place, r.load_sems)

    tags = Spread(place, links, r.tags_t, r.x, L // 4)
    memory = Spread(place, links, r.mem_t, r.m, MPAD)
    cotangent = Spread(place, links, r.cot_t, r.cot, L // 4)
    w_self = Gather(place, links, r.w, 0, 2)
    w_cross, w_ffn = (Gather(place, links, r.w, unit, 2) for unit in (4, 8))
    result = Collect(place, links, r.result, r.result_t)
    tags_grad = Collect(place, links, r.tgrad, r.tgrad_t)
    memory_grad = Collect(place, links, r.mgrad, r.mgrad_t)
    lens = Phase(links, r.lens)
    small_near, small_far = Phase(links, r.small.at[0]), Phase(links, r.small.at[pl.ds(0, 2)])
    def group(unit, per, landing, bufs, n, split=False):
        views = [getattr(r, name).at[n] for name in bufs]
        return Halves(place, links, r, unit, landing), Reduce(place, links, r, unit, per, views, split)

    def freed(first, unit):
        return [r.w.at[first + k, pl.ds(unit, 2)] for k in range(2)]

    one, two = ("s1", "t1", "s2", "t2", "s3"), ("r1", "b1", "r2", "b2", "r3")
    h_out, g_out = group(10, 1, [r.s0.at[k] for k in range(2)], one, 0)
    h_mid, g_mid = group(6, 2, [r.r0.at[k] for k in range(2)], two, 0)
    h_cross, g_cross = group(4, 1, freed(0, 8), one, 1)
    h_value, g_value = group(2, 1, freed(2, 8), one, 2)
    h_query, g_query = group(0, 1, freed(2, 10), one, 3, split=True)
    g_small = SmallReduce(place, links, r)
    assert links.used <= SLOTS
    out = Results(r)

    for t in range(4):
        r.lens_own[pl.ds(t, 1), :] = jnp.full((1, 128), r.tag_lengths[t], jnp.int32)
        r.lens_own[pl.ds(4 + t, 1), :] = jnp.full((1, 128), r.mem_lengths[t], jnp.int32)
    r.small[place.mp, pl.ds(0, 2), :] = r.self_qv_bias[...].astype(F32)
    r.small[place.mp, pl.ds(2, 2), :] = r.cross_qv_bias[...].astype(F32)
    r.small[place.mp, pl.ds(4, 2), :] = r.ffn_in_bias[...].astype(F32)
    r.small[place.mp, pl.ds(6, 2), :] = jnp.zeros((2, 128), F32)
    for n, part in enumerate((r.out_bias, r.norm_gain, r.norm_bias)):
        r.pvec[pl.ds(3 * n, 3), :] = part[...].astype(F32)
    first_loads[0].wait()
    by_table(r.tags_t, r.tags_p)
    greet_wait(place)
    for copy in loads[0]:
        copy.wait()
    w_self.start()
    tags.start()
    lens.send(r.lens_own, r.lens, place.device(lo=1 - place.lo))
    w_self.start_near()
    own = r.small.at[place.mp]
    small_near.send(own, own, place.sibling())
    for core in (place.core, 1 - place.core):
        small_far.send(own, own, place.device(lo=1 - place.lo, hi=1 - place.hi, core=core))
    for copy in loads[1] + loads[2]:
        copy.wait()
    r.w[place.mp, pl.ds(5, 2)] = jnp.swapaxes(r.kv_pairs[...], 0, 1)
    w_cross.start()
    w_ffn.start()
    w_self.step_first()
    first_loads[1].wait()
    r.mem_p[pl.ds(MLOC, MPAD - MLOC)] = jnp.zeros((MPAD - MLOC, 4, D), BF)
    by_table(r.mem_t, r.mem_p)
    memory.start()
    w_cross.start_near()
    w_ffn.start_near()
    w_self.step_second()
    first_loads[2].wait()
    by_table(r.cot_t, r.cot_p)
    cotangent.start()
    w_cross.step_first()
    lens.wait()
    stage_self_mask(r)

    small_near.wait()
    w_self.near.wait()
    tags.wait()
    stage_qkv(r, place.hi)
    w_self.step_last()
    w_cross.step_second()
    w_ffn.step_first()
    stage_self(r, place.hi)
    small_far.wait()
    w_self.far.wait()
    stage_qkv(r, 1 - place.hi)
    w_cross.step_last()
    w_ffn.step_second()
    stage_self(r, 1 - place.hi)
    stage_first(r)
    w_cross.near.wait()
    w_cross.far.wait()
    stage_cross_mask(r)
    stage_cross_q(r)
    memory.wait()
    stage_cross_kv(r)
    w_ffn.step_last()
    stage_cross(r)
    w_ffn.near.wait()
    w_ffn.far.wait()
    kept = stage_rows(r, cotangent.wait)
    links.finish()
    result.start()
    stage_ffn_out_grads(r)
    h_out.start(0)
    h_out.start(1)
    stage_rows_back(r, kept)
    stage_ffn_grads(r)
    h_out.add(g_out, 0)
    h_out.add(g_out, 1)
    g_out.step_plane()
    stage_cross_out_grad(r)
    stage_cross_values(r)
    stage_cross_value_grads(r)
    h_mid.start(0)
    h_mid.start(1)
    stage_cross_back(r, 0)
    g_out.step_line()
    h_mid.add(g_mid, 0)
    stage_cross_back(r, 1)
    h_mid.add(g_mid, 1)
    g_mid.step_plane()
    g_out.step_z()
    stage_memory_grad(r)
    memory_grad.start()
    stage_cross_grads(r)
    h_cross.start(0)
    h_cross.start(1)
    g_out.step_spread()
    stage_first_back(r)
    stage_self_out_grad(r)
    stage_self_values(r)
    h_value.start(0)
    h_value.start(1)
    h_cross.add(g_cross, 0)
    h_cross.add(g_cross, 1)
    g_cross.step_plane()
    g_out.step_spread_more()
    stage_self_back(r, 0)
    g_mid.step_line()
    stage_self_grads(r, 0)
    h_query.start(0)
    h_value.add(g_value, 0)
    h_value.add(g_value, 1)
    g_value.step_plane()
    stage_self_back(r, 1)
    g_cross.step_line()
    g_mid.step_z()
    stage_self_grads(r, 1)
    h_query.start(1)
    g_small.start()
    h_query.add(g_query, 0)
    g_query.step_plane(0)
    stage_tags_grad(r)
    tags_grad.start()
    g_mid.step_spread()
    h_query.add(g_query, 1)
    g_query.step_plane(1)
    g_small.step_x()
    g_cross.step_z()
    g_value.step_line()
    g_out.wait()
    out.units(10, 2)
    result.wait()
    out.rows(r.result_t, r.tags_p, r.result_out)
    g_small.step_y()
    g_query.step_line()
    g_cross.step_spread()
    g_value.step_z()
    g_mid.step_spread_more()
    g_small.step_z()
    memory_grad.wait()
    out.rows(r.mgrad_t, r.mem_p, r.mgrad_out, MLOC)
    g_query.step_z()
    g_value.step_spread()
    g_cross.step_spread_more()
    g_small.wait()
    g_query.step_spread()
    g_value.step_spread_more()
    g_mid.wait()
    out.units(6, 4)
    g_query.step_spread_more()
    g_cross.wait()
    out.units(4, 2)
    tags_grad.wait()
    out.rows(r.tgrad_t, r.cot_p, r.tgrad_out)
    g_value.wait()
    out.units(2, 2)
    g_query.wait()
    out.units(0, 2)
    out.finish()
    links.finish()


def deliver(arrays, outs):
    plain = [name for name in outs if name in arrays]
    made = [name for name in outs if name not in arrays]
    names = plain + ["fin_out"]

    def kernel(*refs):
        refs = list(refs)
        sems = refs.pop()
        srcs = dict(zip(names, refs))
        dsts = dict(zip(outs, refs[len(names) :]))
        held = dict(zip(names + made, refs[len(names) + len(outs) :]))
        reads = {}
        for n, name in enumerate(plain):
            reads[name] = pltpu.make_async_copy(srcs[name], held[name], sems.at[0, n])
            reads[name].start()
        fin = held["fin_out"]
        for n in range(3):
            span = pl.ds(4 * n, 4)
            reads[n] = pltpu.make_async_copy(srcs["fin_out"].at[span], fin.at[span], sems.at[0, len(plain) + n])
            reads[n].start()
        writes = []

        def write(name):
            copy = pltpu.make_async_copy(held[name], dsts[name], sems.at[1, len(writes)])
            copy.start()
            writes.append(copy)

        def blocks(name, first, unit):
            for j in range(4):
                part = fin[unit, pl.ds(j * 128, 128), :].astype(F32)
                held[name][pl.ds(first, 128), pl.ds(j * 128, 128)] = part

        for name in plain:
            reads[name].wait()
            write(name)
        reads[0].wait()
        for j in range(3):
            held["gself_qkv_out"][j] = fin[j].astype(F32)
        write("gself_qkv_out")
        blocks("gself_out_out", 0, 3)
        write("gself_out_out")
        reads[1].wait()
        held["gcross_q_out"][...] = fin[4].astype(F32)
        write("gcross_q_out")
        held["gcross_kv_out"][...] = jnp.swapaxes(fin[pl.ds(5, 2)].astype(F32), 0, 1)
        write("gcross_kv_out")
        blocks("gcross_out_out", 0, 7)
        write("gcross_out_out")
        reads[2].wait()
        for i in range(2):
            held["gffn_in_out"][:, pl.ds(i * 128, 128)] = fin[8 + i].astype(F32)
        write("gffn_in_out")
        for i in range(2):
            blocks("gffn_out_out", i * 128, 10 + i)
        write("gffn_out_out")
        for copy in writes:
            copy.wait()

    hbm = pl.BlockSpec(memory_space=pltpu.HBM)
    shapes = [arrays[name] for name in names] + [outs[name] for name in made]
    return pl.pallas_call(
        kernel,
        out_shape=tuple(outs.values()),
        in_specs=[hbm] * len(names),
        out_specs=(hbm,) * len(outs),
        scratch_shapes=[pltpu.VMEM(a.shape, a.dtype) for a in shapes] + [pltpu.SemaphoreType.DMA((2, len(outs)))],
        compiler_params=pltpu.CompilerParams(vmem_limit_bytes=62 * 1024 * 1024),
        name="deliver",
    )(*[arrays[name] for name in names])


SLOTS = 80


def per_device(
    tags,
    memory,
    cotangent,
    tag_lengths,
    mem_lengths,
    self_qkv,
    self_qv_bias,
    self_out,
    cross_q,
    cross_kv,
    cross_qv_bias,
    cross_out,
    ffn_in,
    ffn_in_bias,
    ffn_out,
    out_bias,
    norm_gain,
    norm_bias,
):
    ins = dict(
        tags=tags,
        memory=memory,
        cotangent=cotangent,
        tag_lengths=tag_lengths,
        mem_lengths=mem_lengths,
        self_qkv=jnp.transpose(self_qkv, (1, 0, 2)),
        self_qv_bias=self_qv_bias,
        self_out=self_out,
        cross_q=cross_q,
        cross_kv=cross_kv,
        cross_qv_bias=cross_qv_bias,
        cross_out=cross_out,
        ffn_in=ffn_in,
        ffn_in_bias=ffn_in_bias.reshape(2, 128),
        ffn_out=ffn_out,
        out_bias=out_bias,
        norm_gain=norm_gain,
        norm_bias=norm_bias,
    )
    in_smem = ("tag_lengths", "mem_lengths")
    in_vmem = ("self_qv_bias", "cross_qv_bias", "ffn_in_bias", "out_bias", "norm_gain", "norm_bias")

    def shape(*dims, dtype=F32):
        return jax.ShapeDtypeStruct(dims, dtype)

    outs = dict(
        result_out=shape(L // 4, 4, D, dtype=BF),
        tgrad_out=shape(L // 4, 4, D, dtype=BF),
        mgrad_out=shape(MLOC, 4, D, dtype=BF),
        gself_qkv_out=shape(3, D, 128),
        gself_qv=shape(2, 128),
        gself_out_out=shape(128, D),
        gcross_q_out=shape(D, 128),
        gcross_kv_out=shape(D, 2, 128),
        gcross_qv=shape(2, 128),
        gcross_out_out=shape(128, D),
        gffn_in_out=shape(D, 256),
        gffn_bias=shape(2, 128),
        gffn_out_out=shape(256, D),
        gout_bias=shape(3, 128),
        gnorm_gain=shape(3, 128),
        gnorm_bias=shape(3, 128),
    )
    own_outs = {name: outs[name] for name in ("result_out", "tgrad_out", "mgrad_out") + SMALL_OUTS}
    own_outs["fin_out"] = shape(12, D, 128, dtype=BF)
    vm = pltpu.VMEM
    scratch = scratch_list()
    scratch.update(
        x=vm((L, D), BF), m=vm((MT, D), BF), cot=vm((L, D), BF),
        lens=vm((8, 128), jnp.int32), lens_own=vm((8, 128), jnp.int32),
        w=vm((4, 12, D, 128), BF), small=vm((4, 8, 128), F32), pvec=vm((16, D), F32),
        tags_p=vm((L // 4, 4, D), BF), mem_p=vm((MPAD, 4, D), BF), cot_p=vm((L // 4, 4, D), BF),
        result=vm((4, L // 4, D), BF), tags_t=vm((4, L // 4, D), BF), mem_t=vm((MT, D), BF), cot_t=vm((4, L // 4, D), BF),
        result_t=vm((4, L // 4, D), BF), mgrad_t=vm((4, MPAD, D), BF), tgrad_t=vm((4, L // 4, D), BF),
        kv_pairs=vm((D, 2, 128), BF), fin=vm((12, D, 128), BF),
        grads=vm((2, 2, 12, D, 128), BF), sums=vm((16, D), F32), bsums=vm((4, 8, 128), F32),
        r0=vm((2, 4, D, 128), BF),
        r1=vm((1, 2, 3, 2, 2, 128, 128), BF), b1=vm((1, 2, 2, 2, 128, 128), BF),
        r2=vm((1, 2, 3, 2, 2, 32, 128), BF), b2=vm((1, 2, 2, 2, 32, 128), BF), r3=vm((1, 3, 2, 2, 32, 128), BF),
        s0=vm((2, 2, D, 128), BF), s1=vm((4, 2, 3, 2, 1, 128, 128), BF), t1=vm((4, 2, 2, 1, 128, 128), BF),
        s2=vm((4, 2, 3, 2, 1, 32, 128), BF), t2=vm((4, 2, 2, 1, 32, 128), BF), s3=vm((4, 3, 2, 1, 32, 128), BF),
        sm=vm((2, 2, 16, 128), F32), sm0=vm((2, 16, 128), F32),
        smx=vm((4, 2, 16, 128), F32), smy=vm((4, 2, 16, 128), F32), smz=vm((4, 2, 16, 128), F32),
        send_sems=pltpu.SemaphoreType.DMA((SLOTS,)),
        recv_sems=pltpu.SemaphoreType.DMA((SLOTS,)),
        load_sems=pltpu.SemaphoreType.DMA((LOADS,)),
        out_sems=pltpu.SemaphoreType.DMA((16,)),
    )
    names = tuple(ins) + tuple(own_outs) + tuple(scratch)
    anywhere = pl.BlockSpec(memory_space=pl.ANY)
    on_chip = pl.BlockSpec(memory_space=pltpu.VMEM)

    def kernel(*refs):
        layer_kernel(Refs(**dict(zip(names, refs))))

    def space(name):
        if name in in_smem:
            return pl.BlockSpec(memory_space=pltpu.SMEM)
        return on_chip if name in in_vmem + SMALL_OUTS else anywhere

    results = pl.pallas_call(
        kernel,
        out_shape=tuple(own_outs.values()),
        in_specs=[space(name) for name in ins],
        out_specs=tuple(space(name) for name in own_outs),
        scratch_shapes=list(scratch.values()),
        compiler_params=pltpu.CompilerParams(
            vmem_limit_bytes=62 * 1024 * 1024, collective_id=0, has_side_effects=True
        ),
        name="layer",
    )(*ins.values())
    results = deliver(dict(zip(own_outs, results)), outs)
    results = dict(zip(outs, results))
    results["gself_qkv_out"] = jnp.transpose(results["gself_qkv_out"], (1, 0, 2))
    results["gffn_bias"] = results["gffn_bias"].reshape(256)
    return tuple(results.values())


def solution(mesh):
    return jax.shard_map(
        per_device,
        mesh=mesh,
        in_specs=(
            P("mp", "dp", None),
            P("mp", "dp", None),
            P("mp", "dp", None),
            P("dp"),
            P("dp"),
            P(None, None, "mp"),
            P(None, "mp"),
            P("mp", None),
            P(None, "mp"),
            P(None, None, "mp"),
            P(None, "mp"),
            P("mp", None),
            P(None, "mp"),
            P("mp"),
            P("mp", None),
            P(),
            P(),
            P(),
        ),
        out_specs=(
            P("mp", "dp", None),
            P("mp", "dp", None),
            P("mp", "dp", None),
            P(None, None, "mp"),
            P(None, "mp"),
            P("mp", None),
            P(None, "mp"),
            P(None, None, "mp"),
            P(None, "mp"),
            P("mp", None),
            P(None, "mp"),
            P("mp"),
            P("mp", None),
            P(None, "mp"),
            P(None, "mp"),
            P(None, "mp"),
        ),
        check_vma=False,
    )
```
